256 devices in a mesh: seq: 8 (over y, core), head: 8 (over z), dp: 4 (over x).
Axes of the slice: x: 4, y: 4, z: 8, core: 2. Of those that a mesh axis runs over, the one named last changes fastest.
Arguments:
- queries: bfloat16 [9216, 8192], P(('dp', 'seq', 'head')), parts along dimension 0, may hold values from -20 to 20
- routed_keys: bfloat16 [9216, 1024], P(('dp', 'seq', 'head')), parts along dimension 0, may hold values from -4 to 4
- routed_values: bfloat16 [9216, 1024], P(('dp', 'seq', 'head')), parts along dimension 0, may hold values from -6 to 6
- output_gradient: bfloat16 [9216, 8192], P(('dp', 'seq', 'head')), parts along dimension 0, may hold values from -6 to 6
- positions: int32 [9216], P('dp'), parts along dimension 0, may hold values from 0 to 12287, as said below
- counts: int32 [32], P('dp'), parts along dimension 0, may hold values from 1 to 288, as said below
Outputs:
- attended: bfloat16 [9216, 8192], P(('dp', 'seq', 'head')), parts along dimension 0
- grad_query: bfloat16 [9216, 8192], P(('dp', 'seq', 'head')), parts along dimension 0
- key_state_gradient: bfloat16 [9216, 1024], P(('dp', 'seq', 'head')), parts along dimension 0
- value_state_gradient: bfloat16 [9216, 1024], P(('dp', 'seq', 'head')), parts along dimension 0
The draws below stay inside these ranges and needn't reach their ends.
There are 4 independent parts, one for each index of `dp`. The reference program is written for one: setup_inputs(seed, part) draws one part's arguments, and reference() takes and returns one part's arrays. A program takes and returns all parts, laid end to end along the dimension named above; each array names one. Nothing has to cross between parts.
Inputs may be any that keep to these rules, and one draw needn't show every extreme that they name: `counts`: one sequence shard has exactly 288; every other shard has 96 or more. Within shard s all positions lie in s * 1536 to (s + 1) * 1536 - 1 and are distinct; the live slots of a shard are strictly increasing.
All inputs are finite; a program needn't handle non-finite values.
Results may differ from the reference program's by a relative error of at most 0.018.
Values may be sent and summed in bfloat16 or wider, within the bound.
A program may use at most 128 MiB of HBM per device.

```python
import jax
import jax.numpy as jnp
from jax import lax

QUERY_HEADS = 64
KEY_VALUE_HEADS = 8
HEAD_WIDTH = 128
TOK_SHARD = 1536
CAP = 288
ROUTED_SLOTS = 2304
N_SEQ = 8


def routed_counts(key, part):
    shard_total = N_SEQ
    other_count = shard_total - 1
    low_count = CAP // 3
    spread_steps = (CAP - low_count) // 4
    first_step = jax.random.randint(jax.random.fold_in(key, 23), (), 0, spread_steps)
    first_share = low_count + jnp.asarray(part, jnp.int32) % 4 + 4 * first_step
    shares = jax.random.randint(jax.random.fold_in(key, 21), (other_count,), low_count, CAP + 1)
    shares = shares.at[0].set(first_share)
    big_shard = jax.random.randint(jax.random.fold_in(key, 22), (), 0, shard_total)
    every_index = jnp.arange(shard_total)
    source_index = jnp.clip(every_index - (every_index > big_shard).astype(jnp.int32), 0, other_count - 1)
    return jnp.where(every_index == big_shard, CAP, shares[source_index]).astype(jnp.int32)


def draw_counts(key, part):
    shared = routed_counts(key, part)
    return shared


def draw_positions(key, part):
    shard_counts = routed_counts(key, part)
    key = jax.random.fold_in(key, 7)
    shard_keys = jax.random.split(key, N_SEQ)
    orders = jax.vmap(lambda one_key: jax.random.permutation(one_key, TOK_SHARD))(shard_keys)
    picked_rows = orders[:, :CAP].astype(jnp.int32)
    slot_index = jnp.arange(CAP)
    is_live = slot_index[None, :] < shard_counts[:, None]
    order_key = jnp.where(is_live, picked_rows, picked_rows + TOK_SHARD)
    sorted_keys = jnp.sort(order_key, axis=1)
    within = jnp.where(sorted_keys >= TOK_SHARD, sorted_keys - TOK_SHARD, sorted_keys)
    placed = within + jnp.arange(N_SEQ, dtype=jnp.int32)[:, None] * TOK_SHARD
    return placed.reshape(ROUTED_SLOTS).astype(jnp.int32)


def draw_routed_keys(key, part):
    key = jax.random.fold_in(key, 3)
    unrotated_input = jax.random.truncated_normal(key, -4.0, 4.0, (ROUTED_SLOTS, KEY_VALUE_HEADS * HEAD_WIDTH), jnp.float32)
    return unrotated_input.astype(jnp.bfloat16)


def draw_queries(key, part):
    key = jax.random.fold_in(key, 4)
    unrotated_input = jax.random.truncated_normal(key, -4.0, 4.0, (ROUTED_SLOTS, QUERY_HEADS * HEAD_WIDTH), jnp.float32)
    return unrotated_input.astype(jnp.bfloat16)


def level_of(own_key, dims, cuts, low, high):
    def one(dim, shards_of):
        heights = jax.random.uniform(jax.random.fold_in(jax.random.fold_in(own_key, 6), dim), (shards_of,), jnp.float32, low / len(cuts), high / len(cuts))
        return jnp.repeat(jnp.exp(heights), dims[dim] // shards_of).reshape((-1,) + (1,) * (len(dims) - dim - 1))

    loudness = one(*cuts[0])
    for cut in cuts[1:]:
        loudness = loudness * one(*cut)
    return loudness


def gaussian(stream_key, extent, spread, most, shards=(), kind=jnp.bfloat16):
    values = jax.random.normal(stream_key, extent, jnp.float32) * spread
    if len(shards) > 0:
        values = level_of(stream_key, extent, shards, -0.22, 0.18) * values
    return jnp.clip(values, min=-most, max=most).astype(kind)


def setup_inputs(seed: int = 0, part: int = 0) -> dict:
    arg_keys = jax.random.split(jax.random.key(seed), 7)
    own_keys = jax.random.split(jax.random.fold_in(arg_keys[6], part), 7)
    return {
        "queries": draw_queries(jax.random.fold_in(jax.random.fold_in(arg_keys[6], part), 71), part),
        "routed_keys": draw_routed_keys(jax.random.fold_in(jax.random.fold_in(arg_keys[6], part), 71), part),
        "routed_values": gaussian(own_keys[2], (ROUTED_SLOTS, KEY_VALUE_HEADS * HEAD_WIDTH), 1.0, 6.0, ((0, 64),)),
        "output_gradient": gaussian(own_keys[3], (ROUTED_SLOTS, QUERY_HEADS * HEAD_WIDTH), 1.0, 6.0, ((0, 64),)),
        "positions": draw_positions(jax.random.fold_in(jax.random.fold_in(arg_keys[6], part), 71), part),
        "counts": draw_counts(jax.random.fold_in(jax.random.fold_in(arg_keys[6], part), 71), part),
    }


ROPE_BASE = 500000.0

def rope_angles(position):
    inverse_freq = jnp.float32(ROPE_BASE) ** (-(jnp.arange(HEAD_WIDTH // 2, dtype=jnp.float32) * 2.0 / HEAD_WIDTH))
    angle_table = position.astype(jnp.float32)[:, None] * inverse_freq[None, :]
    return (jnp.cos(angle_table), jnp.sin(angle_table))

def apply_rotary(vectors, cosine_table, sine_values):
    half_size = vectors.shape[-1] // 2
    lower_half = vectors[..., :half_size]
    upper_half = vectors[..., half_size:]
    cosine_table = cosine_table[:, None, :]
    sine_values = sine_values[:, None, :]
    return jnp.concatenate([lower_half * cosine_table - upper_half * sine_values, upper_half * cosine_table + lower_half * sine_values], -1)

def invert_rotary(vectors, cosine_table, sine_values):
    half_size = vectors.shape[-1] // 2
    lower_half = vectors[..., :half_size]
    upper_half = vectors[..., half_size:]
    cosine_table = cosine_table[:, None, :]
    sine_values = sine_values[:, None, :]
    return jnp.concatenate([lower_half * cosine_table + upper_half * sine_values, upper_half * cosine_table - lower_half * sine_values], -1)

def round_trip(values_in):
    return lax.optimization_barrier(values_in.astype(jnp.bfloat16)).astype(jnp.float32)

def reference(queries, routed_keys, routed_values, output_gradient, positions, counts):
    routed_count = positions.shape[0]
    capacity = routed_count // N_SEQ
    heads_per_group = QUERY_HEADS // KEY_VALUE_HEADS
    score_scale = 1.0 / jnp.sqrt(jnp.float32(HEAD_WIDTH))
    is_valid = jnp.arange(routed_count) % capacity < jnp.repeat(counts, capacity, total_repeat_length=routed_count)
    query_live = is_valid.astype(jnp.float32)
    cosine_table, sine_values = rope_angles(positions)
    query_rotated = apply_rotary(queries.astype(jnp.float32).reshape(routed_count, QUERY_HEADS, HEAD_WIDTH), cosine_table, sine_values).astype(jnp.bfloat16)
    key_rotated = apply_rotary(routed_keys.astype(jnp.float32).reshape(routed_count, KEY_VALUE_HEADS, HEAD_WIDTH), cosine_table, sine_values).astype(jnp.bfloat16)
    allowed = (positions[None, :] <= positions[:, None]) & is_valid[None, :]

    def attend_group(pieces):
        query_group, key_group, value_group, grad_group = pieces
        query_f = query_group.astype(jnp.float32)
        key_f = key_group.astype(jnp.float32)
        value_f = value_group.astype(jnp.float32)
        grad_f = grad_group.astype(jnp.float32)
        scores = jnp.einsum('qhd,kd->hqk', query_f, key_f) * score_scale
        scores = jnp.where(allowed[None], scores, -1e+30)
        row_max = lax.optimization_barrier(jnp.max(scores, -1, keepdims=True))
        weights = jnp.exp(scores - row_max)
        probs = weights / lax.optimization_barrier(jnp.sum(weights, -1, keepdims=True)) * query_live[None, :, None]
        probs_low = round_trip(probs)
        attended = jnp.einsum('hqk,kd->qhd', probs_low, value_f).astype(jnp.bfloat16)
        dprob = jnp.einsum('qhd,kd->hqk', grad_f, value_f)
        delta = lax.optimization_barrier(jnp.sum(grad_f * lax.optimization_barrier(attended).astype(jnp.float32), -1)).T
        dscore = round_trip(probs * (dprob - delta[:, :, None]))
        grad_q = jnp.einsum('hqk,kd->qhd', dscore, key_f) * score_scale
        key_gradient = jnp.einsum('hqk,qhd->kd', dscore, query_f) * score_scale
        value_gradient = jnp.einsum('hqk,qhd->kd', probs_low, grad_f)
        return (attended, grad_q, key_gradient, value_gradient)
    grouped_queries = query_rotated.reshape(routed_count, KEY_VALUE_HEADS, heads_per_group, HEAD_WIDTH).transpose(1, 0, 2, 3)
    gradient_groups = output_gradient.reshape(routed_count, KEY_VALUE_HEADS, heads_per_group, HEAD_WIDTH).transpose(1, 0, 2, 3)
    key_groups = key_rotated.transpose(1, 0, 2)
    grouped_values = routed_values.reshape(routed_count, KEY_VALUE_HEADS, HEAD_WIDTH).transpose(1, 0, 2)
    attended, grad_q, key_gradient, value_gradient = lax.map(attend_group, (grouped_queries, key_groups, grouped_values, gradient_groups))
    attended = attended.transpose(1, 0, 2, 3).reshape(routed_count, QUERY_HEADS * HEAD_WIDTH)
    grad_q = grad_q.transpose(1, 0, 2, 3).reshape(routed_count, QUERY_HEADS, HEAD_WIDTH)
    grad_query = invert_rotary(grad_q, cosine_table, sine_values).astype(jnp.bfloat16).reshape(routed_count, QUERY_HEADS * HEAD_WIDTH)
    key_state_gradient = invert_rotary(key_gradient.transpose(1, 0, 2), cosine_table, sine_values).astype(jnp.bfloat16).reshape(routed_count, KEY_VALUE_HEADS * HEAD_WIDTH)
    value_state_gradient = value_gradient.transpose(1, 0, 2).reshape(routed_count, KEY_VALUE_HEADS * HEAD_WIDTH).astype(jnp.bfloat16)
    return (attended, grad_query, key_state_gradient, value_state_gradient)
```

```python
import functools

import jax
import jax.numpy as jnp
import numpy as np
from jax import lax
from jax.experimental import pallas as pl
from jax.experimental.pallas import tpu as pltpu
from jax.sharding import PartitionSpec as P

QUERY_HEADS = 64
GROUPS = 8
HEADS = 8
WIDTH = 128
NSEQ = 8
NZ = 8
ROWS = 36
CAP = 288
SLOTS = 2304
CHUNK = 384
ROPE_BASE = 500000.0
BIG = 1 << 20
SCALE = 1.0 / np.sqrt(128.0)
SCALE2 = float(SCALE * np.log2(np.e))
MESH = pl.DeviceIdType.MESH
F32 = jnp.float32
BF16 = jnp.bfloat16


def dot_nt(a, b):
    return lax.dot_general(a, b, (((1,), (1,)), ((), ())), preferred_element_type=F32)


def dot_tn(a, b):
    return lax.dot_general(a, b, (((0,), (0,)), ((), ())), preferred_element_type=F32)


def dot_nn(a, b):
    return jnp.dot(a, b, preferred_element_type=F32)


def roll_half(x):
    return pltpu.roll(x, WIDTH // 2, 1)


def rope(x, cos, sin):
    return x * cos + roll_half(x) * sin


def rope_t(x, cos, sin):
    return x * cos - roll_half(x) * sin


HOPS = ((4, 3), (3, 4))


def kernel(
    counts, cos, sin, q_in, k_in, v_in, g_in,
    att_out, dq_out, dk_out, dv_out,
    q_got, g_got, kv_got, kv_ring, stage, q_all, g_all, k_all, v_all, kv_stage,
    slot, limit, s_scr, dk_acc, dv_acc, o_send, dq_send, part, rs_out, rs_in, kv_send,
    sem_kv_s, sem_kv_r, sem_q_s, sem_q_r, sem_g_s, sem_g_r, sem_ag_s, sem_ag_r,
    sem_o_s, sem_o_r, sem_dq_s, sem_dq_r, sem_rs_s, sem_rs_r, sem_b_s, sem_b_r,
):
    me = lax.axis_index("seq")
    mz = lax.axis_index("head")
    right = lax.rem(mz + 1, NZ)
    left = lax.rem(mz + NZ - 1, NZ)
    nbr = (right, left)

    barrier = pltpu.get_barrier_semaphore()
    for d in range(1, NSEQ):
        pl.semaphore_signal(barrier, inc=1, device_id={"seq": lax.rem(me + d, NSEQ)}, device_id_type=MESH)
    for z in nbr:
        pl.semaphore_signal(barrier, inc=1, device_id={"head": z}, device_id_type=MESH)
    pl.semaphore_wait(barrier, NSEQ - 1 + 2)

    def remote(src, dst, ss, rs, **where):
        return pltpu.make_async_remote_copy(
            src_ref=src, dst_ref=dst, send_sem=ss, recv_sem=rs, device_id=where, device_id_type=MESH
        )

    kv_in = (k_in, v_in)

    def kv_copy(i, src, to):
        return remote(
            kv_in[i].at[:, pl.ds(pl.multiple_of(to * WIDTH, WIDTH), WIDTH)],
            kv_got.at[i, src], sem_kv_s.at[i, to], sem_kv_r.at[i, src], seq=to,
        )

    def wide_copy(arr, got, ss, rs, src, to):
        return remote(
            arr.at[:, pl.ds(pl.multiple_of(to * 1024, 1024), 1024)],
            got.at[src], ss.at[to], rs.at[src], seq=to,
        )

    q_copy = functools.partial(wide_copy, q_in, q_got, sem_q_s, sem_q_r)
    g_copy = functools.partial(wide_copy, g_in, g_got, sem_g_s, sem_g_r)
    others = [lax.rem(me + d, NSEQ) for d in range(1, NSEQ)]
    own_kv = [
        pltpu.make_async_copy(
            kv_in[i].at[:, pl.ds(pl.multiple_of(me * WIDTH, WIDTH), WIDTH)], kv_got.at[i, me], sem_kv_r.at[i, me]
        )
        for i in range(2)
    ]
    own_q = pltpu.make_async_copy(
        q_in.at[:, pl.ds(pl.multiple_of(me * 1024, 1024), 1024)], q_got.at[me], sem_q_r.at[me]
    )
    own_g = pltpu.make_async_copy(
        g_in.at[:, pl.ds(pl.multiple_of(me * 1024, 1024), 1024)], g_got.at[me], sem_g_r.at[me]
    )
    for to in others:
        for i in range(2):
            kv_copy(i, me, to).start()
    for c in own_kv:
        c.start()
    own_q.start()
    own_g.start()
    for to in others:
        q_copy(me, to).start()
    for to in others:
        g_copy(me, to).start()

    row_in = lax.broadcasted_iota(jnp.int32, (ROWS, WIDTH), 0) + mz * ROWS
    for h in range(HEADS):
        limit[h * ROWS : (h + 1) * ROWS, :] = row_in
    lane = lax.broadcasted_iota(jnp.int32, (8, SLOTS), 1)
    keep = lane
    for s in range(NSEQ):
        dead = (lane >= s * CAP + counts[s]) & (lane < (s + 1) * CAP)
        keep = jnp.where(dead, BIG, keep)
    slot[...] = keep

    for c in own_kv:
        c.wait()
    for src in others:
        for i in range(2):
            kv_copy(i, src, src).wait_recv()
    for s in range(NSEQ):
        x = rope(kv_got[0, s].astype(F32), cos[s], sin[s])
        kv_stage[0, s * ROWS : (s + 1) * ROWS, :] = x
        kv_stage[1, s * ROWS : (s + 1) * ROWS, :] = kv_got[1, s].astype(F32)
    for i in range(2):
        kv_ring[i, mz] = kv_stage[i].astype(BF16)

    def ag_copy(i, dr, t, z):
        return remote(
            kv_ring.at[i, z], kv_ring.at[i, z], sem_ag_s.at[i, dr, t], sem_ag_r.at[i, dr, t], head=nbr[dr]
        )

    for i in range(2):
        for dr in range(2):
            ag_copy(i, dr, 0, mz).start()

    def place_rows(s):
        for h in range(HEADS):
            cols = slice(h * WIDTH, (h + 1) * WIDTH)
            x = rope(q_got[s, :, cols].astype(F32), cos[s], sin[s])
            stage[0, h * ROWS : (h + 1) * ROWS, :] = x
            stage[1, h * ROWS : (h + 1) * ROWS, :] = g_got[s, :, cols].astype(F32)
        q_all[s] = stage[0].astype(BF16)
        g_all[s] = stage[1].astype(BF16)

    for t in range(4):
        for i in range(2):
            for dr in range(2):
                n = HOPS[i][dr]
                if t < n:
                    step = -(t + 1) if dr == 0 else t + 1
                    z = lax.rem(mz + step + NZ, NZ)
                    ag_copy(i, dr, t, z).wait_recv()
                    if t + 1 < n:
                        ag_copy(i, dr, t + 1, z).start()

    own_q.wait()
    own_g.wait()
    for src in others:
        q_copy(src, src).wait_recv()
        g_copy(src, src).wait_recv()

    def place_step(s, carry):
        place_rows(s)
        return carry

    lax.fori_loop(0, NSEQ, place_step, 0)

    for i, whole in ((0, k_all), (1, v_all)):
        for z in range(NZ):
            x = kv_ring[i, z].astype(F32)
            for s in range(NSEQ):
                part[0, s * CAP + z * ROWS : s * CAP + (z + 1) * ROWS, :] = x[s * ROWS : (s + 1) * ROWS]
        whole[...] = part[0].astype(BF16)

    dk_acc[...] = jnp.zeros_like(dk_acc)
    dv_acc[...] = jnp.zeros_like(dv_acc)

    def out_copy(send, out, ss, rs, src, to):
        return remote(
            send.at[to], out.at[:, pl.ds(pl.multiple_of(src * 1024, 1024), 1024)], ss.at[to], rs.at[src], seq=to
        )

    o_copy = functools.partial(out_copy, o_send, att_out, sem_o_s, sem_o_r)
    dq_copy = functools.partial(out_copy, dq_send, dq_out, sem_dq_s, sem_dq_r)

    def own_out(send, out, rs):
        return pltpu.make_async_copy(
            send.at[me], out.at[:, pl.ds(pl.multiple_of(me * 1024, 1024), 1024)], rs.at[me]
        )

    lanes = CHUNK // WIDTH
    for s in reversed(range(NSEQ)):
        n = ((s + 1) * CAP + CHUNK - 1) // CHUNK
        qb = q_all[s]
        gb = g_all[s]
        lim = limit[...] + s * CAP
        live = (limit[...] < counts[s]).astype(F32)
        top = jnp.full((CAP, WIDTH), -1e30, F32)
        for c in range(n):
            cols = slice(c * CHUNK, (c + 1) * CHUNK)
            sc = dot_nt(qb, k_all[cols, :])
            for t in range(lanes):
                lo = c * CHUNK + t * WIDTH
                x = jnp.where(slot[0:1, lo : lo + WIDTH] <= lim, sc[:, t * WIDTH : (t + 1) * WIDTH], -1e30)
                top = jnp.maximum(top, x)
                s_scr[:, lo : lo + WIDTH] = x
        top = jnp.broadcast_to(jnp.max(top, 1, keepdims=True), (CAP, WIDTH))
        acc = jnp.zeros((CAP, WIDTH), F32)
        total = jnp.zeros((CAP, WIDTH), F32)
        for c in range(n):
            cols = slice(c * CHUNK, (c + 1) * CHUNK)
            ws = []
            for t in range(lanes):
                lo = c * CHUNK + t * WIDTH
                w = jnp.exp2((s_scr[:, lo : lo + WIDTH] - top) * SCALE2)
                s_scr[:, lo : lo + WIDTH] = w
                total = total + w
                ws.append(w.astype(BF16))
            acc = acc + dot_nn(jnp.concatenate(ws, 1), v_all[cols, :])
        inv = live / jnp.sum(total, 1, keepdims=True)
        att = (acc * inv).astype(BF16).astype(F32)
        delta = jnp.sum(gb.astype(F32) * att, 1, keepdims=True)
        delta = jnp.broadcast_to(delta, (CAP, WIDTH))
        for h in range(HEADS):
            o_send[s, :, h * WIDTH : (h + 1) * WIDTH] = att[h * ROWS : (h + 1) * ROWS].astype(BF16)

        @pl.when(me == s)
        def _():
            own_out(o_send, att_out, sem_o_r).start()

        @pl.when(me != s)
        def _():
            o_copy(me, s).start()

        dq = jnp.zeros((CAP, WIDTH), F32)
        for c in range(n):
            cols = slice(c * CHUNK, (c + 1) * CHUNK)
            dp = dot_nt(gb, v_all[cols, :])
            ps, ds = [], []
            for t in range(lanes):
                lo = c * CHUNK + t * WIDTH
                p = s_scr[:, lo : lo + WIDTH] * inv
                ps.append(p.astype(BF16))
                ds.append((p * (dp[:, t * WIDTH : (t + 1) * WIDTH] - delta)).astype(BF16))
            p = jnp.concatenate(ps, 1)
            d = jnp.concatenate(ds, 1)
            dv_acc[cols, :] += dot_tn(p, gb)
            dk_acc[cols, :] += dot_tn(d, qb)
            dq = dq + dot_nn(d, k_all[cols, :])
        dq = dq * SCALE
        for h in range(HEADS):
            x = rope_t(dq[h * ROWS : (h + 1) * ROWS], cos[s], sin[s])
            dq_send[s, :, h * WIDTH : (h + 1) * WIDTH] = x.astype(BF16)

        @pl.when(me == s)
        def _():
            own_out(dq_send, dq_out, sem_dq_r).start()

        @pl.when(me != s)
        def _():
            dq_copy(me, s).start()

    for i, acc in ((0, dk_acc), (1, dv_acc)):
        for z in range(NZ):
            for s in range(NSEQ):
                lo = s * CAP + z * ROWS
                part[i, z * CAP + s * ROWS : z * CAP + (s + 1) * ROWS, :] = acc[lo : lo + ROWS, :]

    def mine(i, z):
        return part[i, pl.ds(pl.multiple_of(z * CAP, CAP), CAP), :]

    def rs_copy(i, dr, t):
        return remote(
            rs_out.at[i, dr, t], rs_in.at[i, dr, t], sem_rs_s.at[i, dr, t], sem_rs_r.at[i, dr, t], head=nbr[dr]
        )

    for t in range(4):
        for i in range(2):
            for dr in range(2):
                n = HOPS[i][dr]
                if t < n:
                    step = n - t if dr == 0 else t - n
                    z = lax.rem(mz + step + NZ, NZ)
                    x = mine(i, z)
                    if t > 0:
                        rs_copy(i, dr, t - 1).wait_recv()
                        x = x + rs_in[i, dr, t - 1].astype(F32)
                    rs_out[i, dr, t] = x.astype(BF16)
                    rs_copy(i, dr, t).start()

    kv_out = (dk_out, dv_out)

    def back_copy(i, src, to):
        return remote(
            kv_send.at[i, to],
            kv_out[i].at[:, pl.ds(pl.multiple_of(src * WIDTH, WIDTH), WIDTH)],
            sem_b_s.at[i, to], sem_b_r.at[i, src], seq=to,
        )

    own_back = [
        pltpu.make_async_copy(
            kv_send.at[i, me],
            kv_out[i].at[:, pl.ds(pl.multiple_of(me * WIDTH, WIDTH), WIDTH)],
            sem_b_r.at[i, me],
        )
        for i in range(2)
    ]
    for i in range(2):
        x = mine(i, mz)
        for dr in range(2):
            n = HOPS[i][dr]
            rs_copy(i, dr, n - 1).wait_recv()
            x = x + rs_in[i, dr, n - 1].astype(F32)
        for s in range(NSEQ):
            y = x[s * ROWS : (s + 1) * ROWS]
            if i == 0:
                y = rope_t(y * SCALE, cos[s], sin[s])
            kv_send[i, s] = y.astype(BF16)
        own_back[i].start()
        for to in others:
            back_copy(i, me, to).start()

    own_out(o_send, att_out, sem_o_r).wait()
    own_out(dq_send, dq_out, sem_dq_r).wait()
    for c in own_back:
        c.wait()
    for src in others:
        o_copy(src, me).wait_recv()
        dq_copy(src, me).wait_recv()
        for i in range(2):
            back_copy(i, src, me).wait_recv()
    for to in others:
        for i in range(2):
            kv_copy(i, me, to).wait_send()
            back_copy(i, me, to).wait_send()
        q_copy(me, to).wait_send()
        g_copy(me, to).wait_send()
        o_copy(me, to).wait_send()
        dq_copy(me, to).wait_send()
    for i in range(2):
        for dr in range(2):
            for t in range(HOPS[i][dr]):
                ag_copy(i, dr, t, mz).wait_send()
                rs_copy(i, dr, t).wait_send()


def shards(queries, routed_keys, routed_values, output_gradient, positions, counts):
    mz = lax.axis_index("head")
    local_pos = lax.dynamic_slice(positions.reshape(NSEQ, CAP), (0, mz * ROWS), (NSEQ, ROWS))
    inverse_freq = jnp.float32(ROPE_BASE) ** (-(jnp.arange(WIDTH // 2, dtype=F32) * 2.0 / WIDTH))
    angle = local_pos.astype(F32)[:, :, None] * inverse_freq
    c, s = jnp.cos(angle), jnp.sin(angle)
    cos = jnp.concatenate([c, c], -1)
    sin = jnp.concatenate([-s, s], -1)
    anywhere = pl.BlockSpec(memory_space=pl.ANY)
    vmem = pl.BlockSpec(memory_space=pltpu.VMEM)
    smem = pl.BlockSpec(memory_space=pltpu.SMEM)
    dma = pltpu.SemaphoreType.DMA
    out = jax.ShapeDtypeStruct
    return pl.pallas_call(
        kernel,
        out_shape=[
            out((ROWS, QUERY_HEADS * WIDTH), BF16),
            out((ROWS, QUERY_HEADS * WIDTH), BF16),
            out((ROWS, GROUPS * WIDTH), BF16),
            out((ROWS, GROUPS * WIDTH), BF16),
        ],
        in_specs=[smem, vmem, vmem, anywhere, anywhere, anywhere, anywhere],
        out_specs=[anywhere] * 4,
        scratch_shapes=[
            pltpu.VMEM((NSEQ, ROWS, HEADS * WIDTH), BF16),
            pltpu.VMEM((NSEQ, ROWS, HEADS * WIDTH), BF16),
            pltpu.VMEM((2, NSEQ, ROWS, WIDTH), BF16),
            pltpu.VMEM((2, NZ, CAP, WIDTH), BF16),
            pltpu.VMEM((2, CAP, WIDTH), F32),
            pltpu.VMEM((NSEQ, CAP, WIDTH), BF16),
            pltpu.VMEM((NSEQ, CAP, WIDTH), BF16),
            pltpu.VMEM((SLOTS, WIDTH), BF16),
            pltpu.VMEM((SLOTS, WIDTH), BF16),
            pltpu.VMEM((2, CAP, WIDTH), F32),
            pltpu.VMEM((8, SLOTS), jnp.int32),
            pltpu.VMEM((CAP, WIDTH), jnp.int32),
            pltpu.VMEM((CAP, SLOTS), F32),
            pltpu.VMEM((SLOTS, WIDTH), F32),
            pltpu.VMEM((SLOTS, WIDTH), F32),
            pltpu.VMEM((NSEQ, ROWS, HEADS * WIDTH), BF16),
            pltpu.VMEM((NSEQ, ROWS, HEADS * WIDTH), BF16),
            pltpu.VMEM((2, SLOTS, WIDTH), F32),
            pltpu.VMEM((2, 2, 4, CAP, WIDTH), BF16),
            pltpu.VMEM((2, 2, 4, CAP, WIDTH), BF16),
            pltpu.VMEM((2, NSEQ, ROWS, WIDTH), BF16),
            dma((2, NSEQ)), dma((2, NSEQ)), dma((NSEQ,)), dma((NSEQ,)), dma((NSEQ,)), dma((NSEQ,)),
            dma((2, 2, 4)), dma((2, 2, 4)),
            dma((NSEQ,)), dma((NSEQ,)), dma((NSEQ,)), dma((NSEQ,)),
            dma((2, 2, 4)), dma((2, 2, 4)), dma((2, NSEQ)), dma((2, NSEQ)),
        ],
        compiler_params=pltpu.CompilerParams(
            collective_id=0, has_side_effects=True, vmem_limit_bytes=48 * 2**20
        ),
        cost_estimate=pl.CostEstimate(flops=5 * 10**9, bytes_accessed=4 * 10**6, transcendentals=3 * 10**6),
    )(counts, cos, sin, queries, routed_keys, routed_values, output_gradient)


def solution(mesh):
    rows = P(("dp", "seq", "head"), None)
    return jax.shard_map(
        shards, mesh=mesh, in_specs=(rows, rows, rows, rows, P("dp"), P("dp")), out_specs=(rows,) * 4, check_vma=False
    )
```

```python
import functools

import jax
import jax.numpy as jnp
import numpy as np
from jax import lax
from jax.experimental import pallas as pl
from jax.experimental.pallas import tpu as pltpu
from jax.sharding import PartitionSpec as P

QUERY_HEADS = 64
GROUPS = 8
HEADS = 8
WIDTH = 128
NSEQ = 8
NZ = 8
ROWS = 36
CAP = 288
SLOTS = 2304
PAIR = 2 * ROWS
WIDEST = 640
ROPE_BASE = 500000.0
BIG = 1 << 20
SCALE = 1.0 / np.sqrt(128.0)
SCALE2 = float(SCALE * np.log2(np.e))
MESH = pl.DeviceIdType.MESH
F32 = jnp.float32
BF16 = jnp.bfloat16


def dot_nt(a, b):
    return lax.dot_general(a, b, (((1,), (1,)), ((), ())), preferred_element_type=F32)


def dot_tn(a, b):
    return lax.dot_general(a, b, (((0,), (0,)), ((), ())), preferred_element_type=F32)


def dot_nn(a, b):
    return jnp.dot(a, b, preferred_element_type=F32)


def roll_half(x):
    return pltpu.roll(x, WIDTH // 2, 1)


def rope(x, cos, sin):
    return x * cos + roll_half(x) * sin


def rope_t(x, cos, sin):
    return x * cos - roll_half(x) * sin


OFFSETS = ((0, -1), (1, -2), (2, -3), (3, 4))
PLACE = {o: (q, w) for q, pair in enumerate(OFFSETS) for w, o in enumerate(pair)}
WIDE = tuple(-(-PAIR * (s + 1) // WIDTH) * WIDTH for s in range(NSEQ))
START = tuple(sum(WIDE[:s]) for s in range(NSEQ))
STORE = sum(WIDE)
FAR, THIRD, SECOND, FIRST = range(4)
DISTANCE = (4, 3, 2, 1)


def kernel(
    pos_in, counts_in, q_in, k_in, v_in, g_in,
    att_out, dq_out, dk_out, dv_out,
    pos, counts, pos_row, cos, sin, q_own, g_own, k_own, v_own,
    q_got, g_got, kv_got, kv_ring, stage, q_all, g_all, pair_stage, k_all, v_all,
    slot, limit, w_all, ds_all, top_all, sum_all, acc_all, inv_all, delta_all, att_all,
    dk_acc, dv_acc, o_send, dq_send, rs_out, rs_in, kv_send,
    sem_p, sem_in, sem_kv_s, sem_kv_r, sem_q_s, sem_q_r, sem_g_s, sem_g_r, sem_ag_s, sem_ag_r,
    sem_o_s, sem_o_r, sem_dq_s, sem_dq_r, sem_rs_s, sem_rs_r, sem_b_s, sem_b_r,
):
    me = lax.axis_index("seq")
    mz = lax.axis_index("head")

    def away(o):
        return lax.rem(mz + (o + NZ), NZ)

    barrier = pltpu.get_barrier_semaphore()
    for d in range(1, NSEQ):
        pl.semaphore_signal(barrier, inc=1, device_id={"seq": lax.rem(me + d, NSEQ)}, device_id_type=MESH)
    for o in (1, -1, 2, -2):
        pl.semaphore_signal(barrier, inc=1, device_id={"head": away(o)}, device_id_type=MESH)
    get_pos = pltpu.make_async_copy(pos_in, pos, sem_p.at[0])
    get_counts = pltpu.make_async_copy(counts_in, counts, sem_p.at[1])
    loads = [
        pltpu.make_async_copy(src, dst, sem_in.at[i])
        for i, (src, dst) in enumerate(((k_in, k_own), (v_in, v_own), (q_in, q_own), (g_in, g_own)))
    ]
    for c in loads:
        c.start()
    get_pos.start()
    get_counts.start()

    def remote(src, dst, ss, rs, **where):
        return pltpu.make_async_remote_copy(
            src_ref=src, dst_ref=dst, send_sem=ss, recv_sem=rs, device_id=where, device_id_type=MESH
        )

    def columns(i, width):
        return pl.ds(pl.multiple_of(i * width, width), width)

    kv_in = (k_own, v_own)

    def kv_copy(i, src, to):
        return remote(
            kv_in[i].at[:, columns(to, WIDTH)], kv_got.at[i, src], sem_kv_s.at[i, to], sem_kv_r.at[i, src], seq=to
        )

    def wide_copy(arr, got, ss, rs, src, to):
        return remote(arr.at[:, columns(to, 1024)], got.at[src], ss.at[to], rs.at[src], seq=to)

    q_copy = functools.partial(wide_copy, q_own, q_got, sem_q_s, sem_q_r)
    g_copy = functools.partial(wide_copy, g_own, g_got, sem_g_s, sem_g_r)
    others = [lax.rem(me + d, NSEQ) for d in range(1, NSEQ)]
    own_kv = [
        pltpu.make_async_copy(kv_in[i].at[:, columns(me, WIDTH)], kv_got.at[i, me], sem_kv_r.at[i, me])
        for i in range(2)
    ]
    own_q = pltpu.make_async_copy(q_own.at[:, columns(me, 1024)], q_got.at[me], sem_q_r.at[me])
    own_g = pltpu.make_async_copy(g_own.at[:, columns(me, 1024)], g_got.at[me], sem_g_r.at[me])
    pl.semaphore_wait(barrier, NSEQ - 1 + 4)
    loads[0].wait()
    loads[1].wait()
    for to in others:
        for i in range(2):
            kv_copy(i, me, to).start()
    for c in own_kv:
        c.start()
    loads[2].wait()
    for to in others:
        q_copy(me, to).start()
    own_q.start()
    loads[3].wait()
    for to in others:
        g_copy(me, to).start()
    own_g.start()

    get_pos.wait()
    get_counts.wait()
    for s in range(NSEQ):
        for r in range(ROWS):
            at = pos[s * CAP + mz * ROWS + r].astype(F32)
            pos_row[s, r : r + 1, :] = jnp.full((1, WIDTH), at, F32)
    lane = lax.broadcasted_iota(jnp.int32, (1, WIDTH), 1)
    upper = lane >= WIDTH // 2
    half = jnp.where(upper, lane - WIDTH // 2, lane).astype(F32)
    freq = jnp.float32(ROPE_BASE) ** (-(half * 2.0 / WIDTH))
    for s in range(NSEQ):
        angle = pos_row[s] * freq
        cos[s] = jnp.cos(angle)
        sine = jnp.sin(angle)
        sin[s] = jnp.where(upper, sine, -sine)
    row_in = lax.broadcasted_iota(jnp.int32, (ROWS, WIDTH), 0) + mz * ROWS
    for h in range(HEADS):
        limit[h * ROWS : (h + 1) * ROWS, :] = row_in
    lane = lax.broadcasted_iota(jnp.int32, (8, WIDEST), 1)
    for q in range(4):
        ids = jnp.full((8, WIDEST), BIG, jnp.int32)
        for w in range(2):
            first = away(OFFSETS[q][w]) * ROWS
            for s in range(NSEQ):
                lo = s * PAIR + w * ROWS
                at = lane - lo + first
                here = (lane >= lo) & (lane < lo + ROWS) & (at < counts[s])
                ids = jnp.where(here, at + s * CAP, ids)
        slot[q] = ids

    def ag_copy(i, dr, t):
        sign = 1 - 2 * dr
        far = t == 3
        src = -2 * sign if far else -sign * t
        dst = 4 if far else -sign * (t + 1)
        return remote(
            kv_ring.at[i, 3 + src], kv_ring.at[i, 3 + dst], sem_ag_s.at[i, dr, t], sem_ag_r.at[i, dr, t],
            head=away(2 * sign if far else sign),
        )

    def ag_all(t):
        return [(i, dr) for i in range(2) for dr in range(2) if t < 3 or i == dr]

    for i in range(2):
        own_kv[i].wait()
        for src in others:
            kv_copy(i, src, src).wait_recv()
        for s in range(NSEQ):
            x = kv_got[i, s].astype(F32)
            if i == 0:
                x = rope(x, cos[s], sin[s])
            stage[s * ROWS : (s + 1) * ROWS, :] = x
        kv_ring[i, 3] = stage[...].astype(BF16)
        for dr in range(2):
            ag_copy(i, dr, 0).start()
    for whole in (k_all, v_all):
        for q in range(4):
            whole[q, NSEQ * PAIR : WIDEST, :] = jnp.zeros((WIDEST - NSEQ * PAIR, WIDTH), BF16)

    def place_q(s):
        for h in range(HEADS):
            x = rope(q_got[s, :, h * WIDTH : (h + 1) * WIDTH].astype(F32), cos[s], sin[s])
            stage[h * ROWS : (h + 1) * ROWS, :] = x
        q_all[s] = stage[...].astype(BF16)

    def place_g(s):
        for h in range(HEADS):
            stage[h * ROWS : (h + 1) * ROWS, :] = g_got[s, :, h * WIDTH : (h + 1) * WIDTH].astype(F32)
        g_all[s] = stage[...].astype(BF16)

    def out_copy(send, out, ss, rs, src, to):
        return remote(send.at[to], out.at[:, columns(src, 1024)], ss.at[to], rs.at[src], seq=to)

    o_copy = functools.partial(out_copy, o_send, att_out, sem_o_s, sem_o_r)
    dq_copy = functools.partial(out_copy, dq_send, dq_out, sem_dq_s, sem_dq_r)

    def own_out(send, out, rs):
        return pltpu.make_async_copy(send.at[me], out.at[:, columns(me, 1024)], rs.at[me])

    def send_back(s, own, copy):
        @pl.when(me == s)
        def _():
            own.start()

        @pl.when(me != s)
        def _():
            copy(me, s).start()

    def forward(q):
        for i, whole in ((0, k_all), (1, v_all)):
            for w in range(2):
                x = kv_ring[i, 3 + OFFSETS[q][w]].astype(F32)
                for s in range(NSEQ):
                    pair_stage[s * PAIR + w * ROWS : s * PAIR + (w + 1) * ROWS, :] = x[s * ROWS : (s + 1) * ROWS]
            whole[q, 0 : NSEQ * PAIR, :] = pair_stage[...].astype(BF16)
        for s in reversed(range(NSEQ)):
            lim = limit[...] + s * CAP
            sc = dot_nt(q_all[s], k_all[q, 0 : WIDE[s], :])
            top = jnp.full((CAP, WIDTH), -1e30, F32)
            xs = []
            for lo in range(0, WIDE[s], WIDTH):
                x = jnp.where(slot[q, 0:1, lo : lo + WIDTH] <= lim, sc[:, lo : lo + WIDTH], -1e30)
                top = jnp.maximum(top, x)
                xs.append(x)
            top = jnp.broadcast_to(jnp.max(top, 1, keepdims=True), (CAP, WIDTH))
            if q > 0:
                before = top_all[q - 1, s]
                top = jnp.maximum(top, before)
            top_all[q, s] = top
            total = jnp.zeros((CAP, WIDTH), F32)
            ws = []
            for n, x in enumerate(xs):
                w = jnp.exp2((x - top) * SCALE2)
                w_all[q, :, START[s] + n * WIDTH : START[s] + (n + 1) * WIDTH] = w
                total = total + w
                ws.append(w.astype(BF16))
            acc = dot_nn(jnp.concatenate(ws, 1), v_all[q, 0 : WIDE[s], :])
            if q > 0:
                shrink = jnp.exp2((before - top) * SCALE2)
                total = total + sum_all[s] * shrink
                acc = acc + acc_all[s] * shrink
            if q < 3:
                sum_all[s] = total
                acc_all[s] = acc
            else:
                live = (limit[...] < counts[s]).astype(F32)
                inv = live / jnp.sum(total, 1, keepdims=True)
                inv_all[s] = inv
                att = (acc * inv).astype(BF16)
                att_all[s] = att
                att = att.astype(F32)
                for h in range(HEADS):
                    o_send[s, :, h * WIDTH : (h + 1) * WIDTH] = att[h * ROWS : (h + 1) * ROWS].astype(BF16)
                send_back(s, own_out(o_send, att_out, sem_o_r), o_copy)

    for t in range(4):
        for i, dr in ag_all(t):
            ag_copy(i, dr, t).wait_recv()
            if t < 2:
                ag_copy(i, dr, t + 1).start()
            if t == 1 and i == dr:
                ag_copy(i, dr, 3).start()
        if t == 0:
            own_q.wait()
            for src in others:
                q_copy(src, src).wait_recv()

            def q_step(s, carry):
                place_q(s)
                return carry

            lax.fori_loop(0, NSEQ, q_step, 0)
        forward(t)

    own_g.wait()
    for src in others:
        g_copy(src, src).wait_recv()

    def g_step(s, carry):
        place_g(s)
        delta = jnp.sum(stage[...] * att_all[s].astype(F32), 1, keepdims=True)
        delta_all[s] = jnp.broadcast_to(delta, (CAP, WIDTH))
        return carry

    lax.fori_loop(0, NSEQ, g_step, 0)

    def backward(q):
        for s in reversed(range(NSEQ)):
            width = WIDE[s]
            qb = q_all[s]
            gb = g_all[s]
            delta = delta_all[s]
            scale = inv_all[s]
            if q < 3:
                scale = scale * jnp.exp2((top_all[q, s] - top_all[3, s]) * SCALE2)
            dp = dot_nt(gb, v_all[q, 0:width, :])
            ps, ds = [], []
            for lo in range(0, width, WIDTH):
                p = w_all[q, :, START[s] + lo : START[s] + lo + WIDTH] * scale
                ps.append(p.astype(BF16))
                d = (p * (dp[:, lo : lo + WIDTH] - delta)).astype(BF16)
                ds_all[q, :, START[s] + lo : START[s] + lo + WIDTH] = d
                ds.append(d)
            dv = dot_tn(jnp.concatenate(ps, 1), gb)
            dk = dot_tn(jnp.concatenate(ds, 1), qb)
            if s == NSEQ - 1:
                dv_acc[q] = dv
                dk_acc[q] = dk
            else:
                dv_acc[q, 0:width, :] += dv
                dk_acc[q, 0:width, :] += dk

    accs = (dk_acc, dv_acc)

    def own_part(i, o, s):
        q, w = PLACE[o]
        return accs[i][q, s * PAIR + w * ROWS : s * PAIR + (w + 1) * ROWS, :]

    def rs_copy(kind, dr, i):
        sign = 1 - 2 * dr
        return remote(
            rs_out.at[kind, dr, i], rs_in.at[kind, dr, i], sem_rs_s.at[kind, dr, i], sem_rs_r.at[kind, dr, i],
            head=away(2 * sign if kind == FAR else sign),
        )

    def rs_kinds(kind, dr):
        return [i for i in range(2) if kind != FAR or i == dr]

    def scatter(kind, dr):
        sign = 1 - 2 * dr
        o = 4 if kind == FAR else sign * DISTANCE[kind]
        for i in rs_kinds(kind, dr):
            adds = []
            if kind == SECOND:
                adds = [THIRD] + ([FAR] if i == dr else [])
            elif kind == FIRST:
                adds = [SECOND]
            for a in adds:
                rs_copy(a, dr, i).wait_recv()
            for s in range(NSEQ):
                x = own_part(i, o, s)
                for a in adds:
                    x = x + rs_in[a, dr, i, s].astype(F32)
                rs_out[kind, dr, i, s] = x.astype(BF16)
            rs_copy(kind, dr, i).start()

    backward(3)
    scatter(THIRD, 0)
    scatter(FAR, 0)
    scatter(FAR, 1)
    backward(2)
    scatter(THIRD, 1)
    backward(1)
    backward(0)
    scatter(SECOND, 0)
    scatter(SECOND, 1)

    for s in reversed(range(NSEQ)):
        dq = jnp.zeros((CAP, WIDTH), F32)
        for q in range(4):
            dq = dq + dot_nn(ds_all[q, :, START[s] : START[s] + WIDE[s]], k_all[q, 0 : WIDE[s], :])
        dq = dq * SCALE
        for h in range(HEADS):
            x = rope_t(dq[h * ROWS : (h + 1) * ROWS], cos[s], sin[s])
            dq_send[s, :, h * WIDTH : (h + 1) * WIDTH] = x.astype(BF16)
        send_back(s, own_out(dq_send, dq_out, sem_dq_r), dq_copy)

    scatter(FIRST, 0)
    scatter(FIRST, 1)

    kv_out = (dk_out, dv_out)

    def back_copy(i, src, to):
        return remote(
            kv_send.at[i, to], kv_out[i].at[:, columns(src, WIDTH)], sem_b_s.at[i, to], sem_b_r.at[i, src], seq=to
        )

    own_back = [
        pltpu.make_async_copy(kv_send.at[i, me], kv_out[i].at[:, columns(me, WIDTH)], sem_b_r.at[i, me])
        for i in range(2)
    ]
    for i in range(2):
        for dr in range(2):
            rs_copy(FIRST, dr, i).wait_recv()
        for s in range(NSEQ):
            x = own_part(i, 0, s)
            for dr in range(2):
                x = x + rs_in[FIRST, dr, i, s].astype(F32)
            if i == 0:
                x = rope_t(x * SCALE, cos[s], sin[s])
            kv_send[i, s] = x.astype(BF16)
            send_back(s, own_back[i], functools.partial(back_copy, i))

    own_out(o_send, att_out, sem_o_r).wait()
    own_out(dq_send, dq_out, sem_dq_r).wait()
    for c in own_back:
        c.wait()
    for src in others:
        o_copy(src, me).wait_recv()
        dq_copy(src, me).wait_recv()
        for i in range(2):
            back_copy(i, src, me).wait_recv()
    for to in others:
        for i in range(2):
            kv_copy(i, me, to).wait_send()
            back_copy(i, me, to).wait_send()
        q_copy(me, to).wait_send()
        g_copy(me, to).wait_send()
        o_copy(me, to).wait_send()
        dq_copy(me, to).wait_send()
    for t in range(4):
        for i, dr in ag_all(t):
            ag_copy(i, dr, t).wait_send()
    for kind in range(4):
        for dr in range(2):
            for i in rs_kinds(kind, dr):
                rs_copy(kind, dr, i).wait_send()


def deliver(*refs):
    held, load_sem, store_sem = refs[8:12], refs[12], refs[13]
    loads = [pltpu.make_async_copy(refs[i], held[i], load_sem.at[i]) for i in range(4)]
    stores = [pltpu.make_async_copy(held[i], refs[i + 4], store_sem.at[i]) for i in range(4)]
    for c in loads:
        c.start()
    for i in range(4):
        loads[i].wait()
        stores[i].start()
    for c in stores:
        c.wait()


def shards(queries, routed_keys, routed_values, output_gradient, positions, counts):
    anywhere = pl.BlockSpec(memory_space=pl.ANY)
    dma = pltpu.SemaphoreType.DMA
    out = jax.ShapeDtypeStruct
    wide = (ROWS, QUERY_HEADS * WIDTH)
    slim = (ROWS, GROUPS * WIDTH)
    results = [out(wide, BF16), out(wide, BF16), out(slim, BF16), out(slim, BF16)]
    by_shard = pltpu.VMEM((NSEQ, CAP, WIDTH), F32)
    found = pl.pallas_call(
        kernel,
        out_shape=results,
        in_specs=[anywhere] * 6,
        out_specs=[anywhere] * 4,
        scratch_shapes=[
            pltpu.SMEM((SLOTS,), jnp.int32),
            pltpu.SMEM((NSEQ,), jnp.int32),
            pltpu.VMEM((NSEQ, ROWS, WIDTH), F32),
            pltpu.VMEM((NSEQ, ROWS, WIDTH), F32),
            pltpu.VMEM((NSEQ, ROWS, WIDTH), F32),
            pltpu.VMEM(wide, BF16),
            pltpu.VMEM(wide, BF16),
            pltpu.VMEM(slim, BF16),
            pltpu.VMEM(slim, BF16),
            pltpu.VMEM((NSEQ, ROWS, HEADS * WIDTH), BF16),
            pltpu.VMEM((NSEQ, ROWS, HEADS * WIDTH), BF16),
            pltpu.VMEM((2, NSEQ, ROWS, WIDTH), BF16),
            pltpu.VMEM((2, NZ, CAP, WIDTH), BF16),
            pltpu.VMEM((CAP, WIDTH), F32),
            pltpu.VMEM((NSEQ, CAP, WIDTH), BF16),
            pltpu.VMEM((NSEQ, CAP, WIDTH), BF16),
            pltpu.VMEM((NSEQ * PAIR, WIDTH), F32),
            pltpu.VMEM((4, WIDEST, WIDTH), BF16),
            pltpu.VMEM((4, WIDEST, WIDTH), BF16),
            pltpu.VMEM((4, 8, WIDEST), jnp.int32),
            pltpu.VMEM((CAP, WIDTH), jnp.int32),
            pltpu.VMEM((4, CAP, STORE), F32),
            pltpu.VMEM((4, CAP, STORE), BF16),
            pltpu.VMEM((4, NSEQ, CAP, WIDTH), F32),
            by_shard,
            by_shard,
            by_shard,
            by_shard,
            pltpu.VMEM((NSEQ, CAP, WIDTH), BF16),
            pltpu.VMEM((4, WIDEST, WIDTH), F32),
            pltpu.VMEM((4, WIDEST, WIDTH), F32),
            pltpu.VMEM((NSEQ, ROWS, HEADS * WIDTH), BF16),
            pltpu.VMEM((NSEQ, ROWS, HEADS * WIDTH), BF16),
            pltpu.VMEM((4, 2, 2, NSEQ, ROWS, WIDTH), BF16),
            pltpu.VMEM((4, 2, 2, NSEQ, ROWS, WIDTH), BF16),
            pltpu.VMEM((2, NSEQ, ROWS, WIDTH), BF16),
            dma((2,)), dma((4,)),
            dma((2, NSEQ)), dma((2, NSEQ)), dma((NSEQ,)), dma((NSEQ,)), dma((NSEQ,)), dma((NSEQ,)),
            dma((2, 2, 4)), dma((2, 2, 4)),
            dma((NSEQ,)), dma((NSEQ,)), dma((NSEQ,)), dma((NSEQ,)),
            dma((4, 2, 2)), dma((4, 2, 2)), dma((2, NSEQ)), dma((2, NSEQ)),
        ],
        compiler_params=pltpu.CompilerParams(
            collective_id=0, has_side_effects=True, vmem_limit_bytes=60 * 2**20
        ),
        cost_estimate=pl.CostEstimate(flops=5 * 10**9, bytes_accessed=4 * 10**6, transcendentals=3 * 10**6),
    )(positions, counts, queries, routed_keys, routed_values, output_gradient)
    return pl.pallas_call(
        deliver,
        out_shape=results,
        in_specs=[anywhere] * 4,
        out_specs=[anywhere] * 4,
        scratch_shapes=[
            pltpu.VMEM(wide, BF16), pltpu.VMEM(wide, BF16), pltpu.VMEM(slim, BF16), pltpu.VMEM(slim, BF16),
            dma((4,)), dma((4,)),
        ],
    )(*found)


def solution(mesh):
    rows = P(("dp", "seq", "head"), None)
    return jax.shard_map(
        shards, mesh=mesh, in_specs=(rows, rows, rows, rows, P("dp"), P("dp")), out_specs=(rows,) * 4, check_vma=False
    )
```

```python
import functools

import jax
import jax.numpy as jnp
import numpy as np
from jax import lax
from jax.experimental import pallas as pl
from jax.experimental.pallas import tpu as pltpu
from jax.sharding import PartitionSpec as P

QUERY_HEADS = 64
GROUPS = 8
HEADS = 8
WIDTH = 128
NSEQ = 8
NZ = 8
ROWS = 36
CAP = 288
SLOTS = 2304
WIDEST = 640
ROPE_BASE = 500000.0
BIG = 1 << 20
SCALE = 1.0 / np.sqrt(128.0)
SCALE2 = float(SCALE * np.log2(np.e))
MESH = pl.DeviceIdType.MESH
F32 = jnp.float32
BF16 = jnp.bfloat16


def dot_nt(a, b):
    return lax.dot_general(a, b, (((1,), (1,)), ((), ())), preferred_element_type=F32)


def dot_tn(a, b):
    return lax.dot_general(a, b, (((0,), (0,)), ((), ())), preferred_element_type=F32)


def dot_nn(a, b):
    return jnp.dot(a, b, preferred_element_type=F32)


def roll_half(x):
    return pltpu.roll(x, WIDTH // 2, 1)


def rope(x, cos, sin):
    return x * cos + roll_half(x) * sin


def rope_t(x, cos, sin):
    return x * cos - roll_half(x) * sin


OFFSETS = ((0,), (1, -1), (2, -2), (3, -3), (4,))
LAST = len(OFFSETS) - 1
PLACE = {o: (q, w) for q, group in enumerate(OFFSETS) for w, o in enumerate(group)}
STEP = tuple(ROWS * len(group) for group in OFFSETS)
WIDE = tuple(tuple(-(-step * (s + 1) // WIDTH) * WIDTH for s in range(NSEQ)) for step in STEP)
START, STORE = [], 0
for _wide in WIDE:
    START.append([])
    for _w in _wide:
        START[-1].append(STORE)
        STORE += _w
FAR, THIRD, SECOND, FIRST = range(4)
DISTANCE = (4, 3, 2, 1)


def kernel(
    pos_in, counts_in, q_in, k_in, v_in, g_in,
    att_out, dq_out, dk_out, dv_out,
    pos, counts, pos_row, cos, sin, q_own, g_own, k_raw, k_own, v_own,
    q_got, g_got, kv_ring, stage, q_all, g_all, pair_stage, k_all, v_all,
    slot, limit, w_all, ds_all, top_all, sum_all, acc_all, inv_all, delta_all, att_all,
    dk_acc, dv_acc, o_send, dq_send, rs_out, rs_in, kv_send,
    sem_p, sem_in, sem_kv_s, sem_kv_r, sem_q_s, sem_q_r, sem_g_s, sem_g_r, sem_ag_s, sem_ag_r,
    sem_o_s, sem_o_r, sem_dq_s, sem_dq_r, sem_rs_s, sem_rs_r, sem_b_s, sem_b_r,
):
    me = lax.axis_index("seq")
    mz = lax.axis_index("head")

    def away(o):
        return lax.rem(mz + (o + NZ), NZ)

    barrier = pltpu.get_barrier_semaphore()
    for d in range(1, NSEQ):
        pl.semaphore_signal(barrier, inc=1, device_id={"seq": lax.rem(me + d, NSEQ)}, device_id_type=MESH)
    for o in (1, -1, 2, -2):
        pl.semaphore_signal(barrier, inc=1, device_id={"head": away(o)}, device_id_type=MESH)
    get_pos = pltpu.make_async_copy(pos_in, pos, sem_p.at[0])
    get_counts = pltpu.make_async_copy(counts_in, counts, sem_p.at[1])
    loads = [
        pltpu.make_async_copy(src, dst, sem_in.at[i])
        for i, (src, dst) in enumerate(((k_in, k_raw), (v_in, v_own), (q_in, q_own), (g_in, g_own)))
    ]
    for c in loads:
        c.start()
    get_pos.start()
    get_counts.start()

    def remote(src, dst, ss, rs, **where):
        return pltpu.make_async_remote_copy(
            src_ref=src, dst_ref=dst, send_sem=ss, recv_sem=rs, device_id=where, device_id_type=MESH
        )

    def columns(i, width):
        return pl.ds(pl.multiple_of(i * width, width), width)

    kv_in = (k_own, v_own)

    def kv_copy(i, src, to):
        return remote(
            kv_in[i].at[:, columns(to, WIDTH)], kv_ring.at[i, 3, src], sem_kv_s.at[i, to], sem_kv_r.at[i, src], seq=to
        )

    def wide_copy(arr, got, ss, rs, src, to):
        return remote(arr.at[:, columns(to, 1024)], got.at[src], ss.at[to], rs.at[src], seq=to)

    q_copy = functools.partial(wide_copy, q_own, q_got, sem_q_s, sem_q_r)
    g_copy = functools.partial(wide_copy, g_own, g_got, sem_g_s, sem_g_r)
    others = [lax.rem(me + d, NSEQ) for d in range(1, NSEQ)]
    own_kv = [
        pltpu.make_async_copy(kv_in[i].at[:, columns(me, WIDTH)], kv_ring.at[i, 3, me], sem_kv_r.at[i, me])
        for i in range(2)
    ]
    own_q = pltpu.make_async_copy(q_own.at[:, columns(me, 1024)], q_got.at[me], sem_q_r.at[me])
    own_g = pltpu.make_async_copy(g_own.at[:, columns(me, 1024)], g_got.at[me], sem_g_r.at[me])
    get_pos.wait()
    for s in range(NSEQ):
        for r in range(ROWS):
            at = pos[s * CAP + mz * ROWS + r].astype(F32)
            pos_row[s, r : r + 1, :] = jnp.full((1, WIDTH), at, F32)
    lane = lax.broadcasted_iota(jnp.int32, (1, WIDTH), 1)
    upper = lane >= WIDTH // 2
    half = jnp.where(upper, lane - WIDTH // 2, lane).astype(F32)
    freq = jnp.float32(ROPE_BASE) ** (-(half * 2.0 / WIDTH))
    for s in range(NSEQ):
        angle = pos_row[s] * freq
        cos[s] = jnp.cos(angle)
        sine = jnp.sin(angle)
        sin[s] = jnp.where(upper, sine, -sine)
    for c in loads:
        c.wait()
    for g in range(GROUPS):
        cols = slice(g * WIDTH, (g + 1) * WIDTH)
        k_own[:, cols] = rope(k_raw[:, cols].astype(F32), cos[me], sin[me]).astype(BF16)
    pl.semaphore_wait(barrier, NSEQ - 1 + 4)
    for i in range(2):
        for to in others:
            kv_copy(i, me, to).start()
        own_kv[i].start()
    for to in others:
        q_copy(me, to).start()
    own_q.start()
    for to in others:
        g_copy(me, to).start()
    own_g.start()

    get_counts.wait()
    row_in = lax.broadcasted_iota(jnp.int32, (ROWS, WIDTH), 0) + mz * ROWS
    for h in range(HEADS):
        limit[h * ROWS : (h + 1) * ROWS, :] = row_in
    lane = lax.broadcasted_iota(jnp.int32, (8, WIDEST), 1)
    for q in range(LAST + 1):
        ids = jnp.full((8, WIDEST), BIG, jnp.int32)
        for w, o in enumerate(OFFSETS[q]):
            first = away(o) * ROWS
            for s in range(NSEQ):
                lo = s * STEP[q] + w * ROWS
                at = lane - lo + first
                here = (lane >= lo) & (lane < lo + ROWS) & (at < counts[s])
                ids = jnp.where(here, at + s * CAP, ids)
        slot[q] = ids

    def ag_copy(i, dr, t):
        sign = 1 - 2 * dr
        far = t == 3
        src = -2 * sign if far else -sign * t
        dst = 4 if far else -sign * (t + 1)
        return remote(
            kv_ring.at[i, 3 + src], kv_ring.at[i, 3 + dst], sem_ag_s.at[i, dr, t], sem_ag_r.at[i, dr, t],
            head=away(2 * sign if far else sign),
        )

    def ag_all(t):
        return [(i, dr) for i in range(2) for dr in range(2) if t < 3 or i == dr]

    for i in range(2):
        own_kv[i].wait()
        for src in others:
            kv_copy(i, src, src).wait_recv()
        for dr in range(2):
            ag_copy(i, dr, 0).start()
    for whole in (k_all, v_all):
        for q in range(LAST + 1):
            rest = WIDEST - NSEQ * STEP[q]
            whole[q, NSEQ * STEP[q] : WIDEST, :] = jnp.zeros((rest, WIDTH), BF16)

    def place_q(s):
        for h in range(HEADS):
            x = rope(q_got[s, :, h * WIDTH : (h + 1) * WIDTH].astype(F32), cos[s], sin[s])
            stage[h * ROWS : (h + 1) * ROWS, :] = x
        q_all[s] = stage[...].astype(BF16)

    def place_g(s):
        for h in range(HEADS):
            stage[h * ROWS : (h + 1) * ROWS, :] = g_got[s, :, h * WIDTH : (h + 1) * WIDTH].astype(F32)
        g_all[s] = stage[...].astype(BF16)

    def out_copy(send, out, ss, rs, src, to):
        return remote(send.at[to], out.at[:, columns(src, 1024)], ss.at[to], rs.at[src], seq=to)

    o_copy = functools.partial(out_copy, o_send, att_out, sem_o_s, sem_o_r)
    dq_copy = functools.partial(out_copy, dq_send, dq_out, sem_dq_s, sem_dq_r)

    def own_out(send, out, rs):
        return pltpu.make_async_copy(send.at[me], out.at[:, columns(me, 1024)], rs.at[me])

    def send_back(own, copy):
        for to in others:
            copy(me, to).start()
        own.start()

    def line_up(i, whole, q):
        for w, o in enumerate(OFFSETS[q]):
            for s in range(NSEQ):
                lo = s * STEP[q] + w * ROWS
                pair_stage[lo : lo + ROWS, :] = kv_ring[i, 3 + o, s].astype(F32)
        whole[q, 0 : NSEQ * STEP[q], :] = pair_stage[0 : NSEQ * STEP[q], :].astype(BF16)

    def weigh(q):
        line_up(0, k_all, q)
        for s in reversed(range(NSEQ)):
            lim = limit[...] + s * CAP
            sc = dot_nt(q_all[s], k_all[q, 0 : WIDE[q][s], :])
            top = jnp.full((CAP, WIDTH), -1e30, F32)
            xs = []
            for lo in range(0, WIDE[q][s], WIDTH):
                x = jnp.where(slot[q, 0:1, lo : lo + WIDTH] <= lim, sc[:, lo : lo + WIDTH], -1e30)
                top = jnp.maximum(top, x)
                xs.append(x)
            top = jnp.broadcast_to(jnp.max(top, 1, keepdims=True), (CAP, WIDTH))
            if q > 0:
                before = top_all[q - 1, s]
                top = jnp.maximum(top, before)
            top_all[q, s] = top
            total = jnp.zeros((CAP, WIDTH), F32)
            for n, x in enumerate(xs):
                w = jnp.exp2((x - top) * SCALE2)
                w_all[:, START[q][s] + n * WIDTH : START[q][s] + (n + 1) * WIDTH] = w
                total = total + w
            if q > 0:
                total = total + sum_all[s] * jnp.exp2((before - top) * SCALE2)
            sum_all[s] = total

    def gather(q):
        line_up(1, v_all, q)
        for s in reversed(range(NSEQ)):
            w = w_all[:, START[q][s] : START[q][s] + WIDE[q][s]].astype(BF16)
            acc = dot_nn(w, v_all[q, 0 : WIDE[q][s], :])
            if q > 0:
                acc = acc + acc_all[s] * jnp.exp2((top_all[q - 1, s] - top_all[q, s]) * SCALE2)
            if q < LAST:
                acc_all[s] = acc
            else:
                live = (limit[...] < counts[s]).astype(F32)
                inv = live / jnp.sum(sum_all[s], 1, keepdims=True)
                inv_all[s] = inv
                att = (acc * inv).astype(BF16)
                att_all[s] = att

    def arrive(t, i):
        for dr in range(2):
            if t < 3 or i == dr:
                ag_copy(i, dr, t).wait_recv()
                if t < 2:
                    ag_copy(i, dr, t + 1).start()
                if t == 1 and i == dr:
                    ag_copy(i, dr, 3).start()

    def q_step(s, carry):
        place_q(s)
        return carry

    arrive(0, 0)
    arrive(0, 1)
    own_q.wait()
    for src in others:
        q_copy(src, src).wait_recv()
    lax.fori_loop(0, NSEQ, q_step, 0)
    weigh(0)
    gather(0)
    arrive(1, 0)
    weigh(1)
    arrive(1, 1)
    gather(1)
    weigh(2)
    gather(2)
    arrive(2, 0)
    weigh(3)
    arrive(2, 1)
    gather(3)

    def g_step(s, carry):
        place_g(s)
        return carry

    own_g.wait()
    for src in others:
        g_copy(src, src).wait_recv()
    lax.fori_loop(0, NSEQ, g_step, 0)
    arrive(3, 0)
    weigh(4)
    arrive(3, 1)
    gather(4)

    def backward(q):
        for s in reversed(range(NSEQ)):
            width = WIDE[q][s]
            qb = q_all[s]
            gb = g_all[s]
            scale = inv_all[s]
            if q == LAST:
                delta = jnp.sum(gb.astype(F32) * att_all[s].astype(F32), 1, keepdims=True)
                delta = jnp.broadcast_to(delta, (CAP, WIDTH))
                delta_all[s] = delta
            else:
                delta = delta_all[s]
                scale = scale * jnp.exp2((top_all[q, s] - top_all[LAST, s]) * SCALE2)
            dp = dot_nt(gb, v_all[q, 0:width, :])
            ps, ds = [], []
            for lo in range(0, width, WIDTH):
                at = START[q][s] + lo
                p = w_all[:, at : at + WIDTH] * scale
                ps.append(p.astype(BF16))
                d = (p * (dp[:, lo : lo + WIDTH] - delta)).astype(BF16)
                ds_all[:, at : at + WIDTH] = d
                ds.append(d)
            dv = dot_tn(jnp.concatenate(ps, 1), gb)
            dk = dot_tn(jnp.concatenate(ds, 1), qb)
            if s == NSEQ - 1:
                dv_acc[q, 0:width, :] = dv
                dk_acc[q, 0:width, :] = dk
            else:
                dv_acc[q, 0:width, :] += dv
                dk_acc[q, 0:width, :] += dk

    accs = (dk_acc, dv_acc)

    def own_part(i, o, s):
        q, w = PLACE[o]
        lo = s * STEP[q] + w * ROWS
        return accs[i][q, lo : lo + ROWS, :]

    def rs_copy(kind, dr, i):
        sign = 1 - 2 * dr
        return remote(
            rs_out.at[kind, dr, i], rs_in.at[kind, dr, i], sem_rs_s.at[kind, dr, i], sem_rs_r.at[kind, dr, i],
            head=away(2 * sign if kind in (FAR, SECOND) else sign),
        )

    def rs_kinds(kind, dr):
        return [i for i in range(2) if kind != FAR or i == dr]

    def scatter(kind, dr):
        sign = 1 - 2 * dr
        o = 4 if kind == FAR else sign * DISTANCE[kind]
        for i in rs_kinds(kind, dr):
            adds = []
            if kind == SECOND:
                adds = [THIRD] + ([FAR] if i == dr else [])
            for a in adds:
                rs_copy(a, dr, i).wait_recv()
            for s in range(NSEQ):
                x = own_part(i, o, s)
                for a in adds:
                    x = x + rs_in[a, dr, i, s].astype(F32)
                rs_out[kind, dr, i, s] = x.astype(BF16)
            rs_copy(kind, dr, i).start()

    backward(4)
    scatter(FAR, 0)
    scatter(FAR, 1)
    for s in range(NSEQ):
        att = att_all[s].astype(F32)
        for h in range(HEADS):
            o_send[s, :, h * WIDTH : (h + 1) * WIDTH] = att[h * ROWS : (h + 1) * ROWS].astype(BF16)
    send_back(own_out(o_send, att_out, sem_o_r), o_copy)
    backward(3)
    scatter(THIRD, 0)
    scatter(THIRD, 1)
    backward(2)
    backward(1)
    scatter(FIRST, 0)
    scatter(FIRST, 1)
    scatter(SECOND, 0)
    scatter(SECOND, 1)
    backward(0)

    for s in reversed(range(NSEQ)):
        dq = jnp.zeros((CAP, WIDTH), F32)
        for q in range(LAST + 1):
            d = ds_all[:, START[q][s] : START[q][s] + WIDE[q][s]]
            dq = dq + dot_nn(d, k_all[q, 0 : WIDE[q][s], :])
        dq = dq * SCALE
        for h in range(HEADS):
            x = rope_t(dq[h * ROWS : (h + 1) * ROWS], cos[s], sin[s])
            dq_send[s, :, h * WIDTH : (h + 1) * WIDTH] = x.astype(BF16)
    send_back(own_out(dq_send, dq_out, sem_dq_r), dq_copy)

    kv_out = (dk_out, dv_out)

    def back_copy(i, src, to):
        return remote(
            kv_send.at[i, to], kv_out[i].at[:, columns(src, WIDTH)], sem_b_s.at[i, to], sem_b_r.at[i, src], seq=to
        )

    own_back = [
        pltpu.make_async_copy(kv_send.at[i, me], kv_out[i].at[:, columns(me, WIDTH)], sem_b_r.at[i, me])
        for i in range(2)
    ]
    for i in range(2):
        ends = [(kind, dr) for kind in (FIRST, SECOND) for dr in range(2)]
        for kind, dr in ends:
            rs_copy(kind, dr, i).wait_recv()
        for s in range(NSEQ):
            x = own_part(i, 0, s)
            for kind, dr in ends:
                x = x + rs_in[kind, dr, i, s].astype(F32)
            if i == 0:
                x = rope_t(x * SCALE, cos[s], sin[s])
            kv_send[i, s] = x.astype(BF16)
        send_back(own_back[i], functools.partial(back_copy, i))

    own_out(o_send, att_out, sem_o_r).wait()
    own_out(dq_send, dq_out, sem_dq_r).wait()
    for c in own_back:
        c.wait()
    for src in others:
        o_copy(src, me).wait_recv()
        dq_copy(src, me).wait_recv()
        for i in range(2):
            back_copy(i, src, me).wait_recv()
    for to in others:
        for i in range(2):
            kv_copy(i, me, to).wait_send()
            back_copy(i, me, to).wait_send()
        q_copy(me, to).wait_send()
        g_copy(me, to).wait_send()
        o_copy(me, to).wait_send()
        dq_copy(me, to).wait_send()
    for t in range(4):
        for i, dr in ag_all(t):
            ag_copy(i, dr, t).wait_send()
    for kind in range(4):
        for dr in range(2):
            for i in rs_kinds(kind, dr):
                rs_copy(kind, dr, i).wait_send()


def deliver(*refs):
    held, load_sem, store_sem = refs[8:12], refs[12], refs[13]
    loads = [pltpu.make_async_copy(refs[i], held[i], load_sem.at[i]) for i in range(4)]
    stores = [pltpu.make_async_copy(held[i], refs[i + 4], store_sem.at[i]) for i in range(4)]
    for c in loads:
        c.start()
    for i in range(4):
        loads[i].wait()
        stores[i].start()
    for c in stores:
        c.wait()


def shards(queries, routed_keys, routed_values, output_gradient, positions, counts):
    anywhere = pl.BlockSpec(memory_space=pl.ANY)
    dma = pltpu.SemaphoreType.DMA
    out = jax.ShapeDtypeStruct
    wide = (ROWS, QUERY_HEADS * WIDTH)
    slim = (ROWS, GROUPS * WIDTH)
    results = [out(wide, BF16), out(wide, BF16), out(slim, BF16), out(slim, BF16)]
    by_shard = pltpu.VMEM((NSEQ, CAP, WIDTH), F32)
    found = pl.pallas_call(
        kernel,
        out_shape=results,
        in_specs=[anywhere] * 6,
        out_specs=[anywhere] * 4,
        scratch_shapes=[
            pltpu.SMEM((SLOTS,), jnp.int32),
            pltpu.SMEM((NSEQ,), jnp.int32),
            pltpu.VMEM((NSEQ, ROWS, WIDTH), F32),
            pltpu.VMEM((NSEQ, ROWS, WIDTH), F32),
            pltpu.VMEM((NSEQ, ROWS, WIDTH), F32),
            pltpu.VMEM(wide, BF16),
            pltpu.VMEM(wide, BF16),
            pltpu.VMEM(slim, BF16),
            pltpu.VMEM(slim, BF16),
            pltpu.VMEM(slim, BF16),
            pltpu.VMEM((NSEQ, ROWS, HEADS * WIDTH), BF16),
            pltpu.VMEM((NSEQ, ROWS, HEADS * WIDTH), BF16),
            pltpu.VMEM((2, NZ, NSEQ, ROWS, WIDTH), BF16),
            pltpu.VMEM((CAP, WIDTH), F32),
            pltpu.VMEM((NSEQ, CAP, WIDTH), BF16),
            pltpu.VMEM((NSEQ, CAP, WIDTH), BF16),
            pltpu.VMEM((NSEQ * max(STEP), WIDTH), F32),
            pltpu.VMEM((LAST + 1, WIDEST, WIDTH), BF16),
            pltpu.VMEM((LAST + 1, WIDEST, WIDTH), BF16),
            pltpu.VMEM((LAST + 1, 8, WIDEST), jnp.int32),
            pltpu.VMEM((CAP, WIDTH), jnp.int32),
            pltpu.VMEM((CAP, STORE), F32),
            pltpu.VMEM((CAP, STORE), BF16),
            pltpu.VMEM((LAST + 1, NSEQ, CAP, WIDTH), F32),
            by_shard,
            by_shard,
            by_shard,
            by_shard,
            pltpu.VMEM((NSEQ, CAP, WIDTH), BF16),
            pltpu.VMEM((LAST + 1, WIDEST, WIDTH), F32),
            pltpu.VMEM((LAST + 1, WIDEST, WIDTH), F32),
            pltpu.VMEM((NSEQ, ROWS, HEADS * WIDTH), BF16),
            pltpu.VMEM((NSEQ, ROWS, HEADS * WIDTH), BF16),
            pltpu.VMEM((4, 2, 2, NSEQ, ROWS, WIDTH), BF16),
            pltpu.VMEM((4, 2, 2, NSEQ, ROWS, WIDTH), BF16),
            pltpu.VMEM((2, NSEQ, ROWS, WIDTH), BF16),
            dma((2,)), dma((4,)),
            dma((2, NSEQ)), dma((2, NSEQ)), dma((NSEQ,)), dma((NSEQ,)), dma((NSEQ,)), dma((NSEQ,)),
            dma((2, 2, 4)), dma((2, 2, 4)),
            dma((NSEQ,)), dma((NSEQ,)), dma((NSEQ,)), dma((NSEQ,)),
            dma((4, 2, 2)), dma((4, 2, 2)), dma((2, NSEQ)), dma((2, NSEQ)),
        ],
        compiler_params=pltpu.CompilerParams(
            collective_id=0, has_side_effects=True, vmem_limit_bytes=60 * 2**20
        ),
        cost_estimate=pl.CostEstimate(flops=5 * 10**9, bytes_accessed=4 * 10**6, transcendentals=3 * 10**6),
    )(positions, counts, queries, routed_keys, routed_values, output_gradient)
    return pl.pallas_call(
        deliver,
        out_shape=results,
        in_specs=[anywhere] * 4,
        out_specs=[anywhere] * 4,
        scratch_shapes=[
            pltpu.VMEM(wide, BF16), pltpu.VMEM(wide, BF16), pltpu.VMEM(slim, BF16), pltpu.VMEM(slim, BF16),
            dma((4,)), dma((4,)),
        ],
    )(*found)


def solution(mesh):
    rows = P(("dp", "seq", "head"), None)
    return jax.shard_map(
        shards, mesh=mesh, in_specs=(rows, rows, rows, rows, P("dp"), P("dp")), out_specs=(rows,) * 4, check_vma=False
    )
```

```python
import functools

import jax
import jax.numpy as jnp
import numpy as np
from jax import lax
from jax.experimental import pallas as pl
from jax.experimental.pallas import tpu as pltpu
from jax.sharding import PartitionSpec as P

QUERY_HEADS = 64
GROUPS = 8
HEADS = 8
WIDTH = 128
NSEQ = 8
NZ = 8
ROWS = 36
CAP = 288
SLOTS = 2304
WIDEST = 640
ROPE_BASE = 500000.0
BIG = 1 << 20
SCALE = 1.0 / np.sqrt(128.0)
SCALE2 = float(SCALE * np.log2(np.e))
MESH = pl.DeviceIdType.MESH
F32 = jnp.float32
BF16 = jnp.bfloat16


def dot_nt(a, b):
    return lax.dot_general(a, b, (((1,), (1,)), ((), ())), preferred_element_type=F32)


def dot_tn(a, b):
    return lax.dot_general(a, b, (((0,), (0,)), ((), ())), preferred_element_type=F32)


def dot_nn(a, b):
    return jnp.dot(a, b, preferred_element_type=F32)


def roll_half(x):
    return pltpu.roll(x, WIDTH // 2, 1)


def rope(x, cos, sin):
    return x * cos + roll_half(x) * sin


def rope_t(x, cos, sin):
    return x * cos - roll_half(x) * sin


OFFSETS = ((0,), (1, -1), (2, -2), (3, -3), (4,))
LAST = len(OFFSETS) - 1
PLACE = {o: (q, w) for q, group in enumerate(OFFSETS) for w, o in enumerate(group)}
STEP = tuple(ROWS * len(group) for group in OFFSETS)
WIDE = tuple(tuple(-(-step * (s + 1) // WIDTH) * WIDTH for s in range(NSEQ)) for step in STEP)
START, STORE = [], 0
for _wide in WIDE:
    START.append([])
    for _w in _wide:
        START[-1].append(STORE)
        STORE += _w
FAR, THIRD, SECOND, FIRST = range(4)
DISTANCE = (4, 3, 2, 1)


def kernel(
    pos_in, counts_in, q_in, k_in, v_in, g_in,
    att_out, dq_out, dk_out, dv_out,
    pos, counts, pos_row, cos, sin, q_own, g_own, k_raw, k_own, v_own,
    q_got, g_got, kv_ring, stage, q_all, g_all, pair_stage, k_all, v_all,
    slot, limit, w_all, ds_all, top_all, sum_all, acc_all, inv_all, delta_all, att_all,
    dk_acc, dv_acc, dk_turned, dv_turned, o_send, dq_send, rs_out, rs_in, kv_send,
    sem_p, sem_in, sem_kv_s, sem_kv_r, sem_q_s, sem_q_r, sem_g_s, sem_g_r, sem_ag_s, sem_ag_r,
    sem_o_s, sem_o_r, sem_dq_s, sem_dq_r, sem_rs_s, sem_rs_r, sem_b_s, sem_b_r,
):
    me = lax.axis_index("seq")
    mz = lax.axis_index("head")

    def away(o):
        return lax.rem(mz + (o + NZ), NZ)

    barrier = pltpu.get_barrier_semaphore()
    for d in range(1, NSEQ):
        pl.semaphore_signal(barrier, inc=1, device_id={"seq": lax.rem(me + d, NSEQ)}, device_id_type=MESH)
    for o in (1, -1, 2, -2):
        pl.semaphore_signal(barrier, inc=1, device_id={"head": away(o)}, device_id_type=MESH)
    get_pos = pltpu.make_async_copy(pos_in, pos, sem_p.at[0])
    get_counts = pltpu.make_async_copy(counts_in, counts, sem_p.at[1])
    loads = [
        pltpu.make_async_copy(src, dst, sem_in.at[i])
        for i, (src, dst) in enumerate(((k_in, k_raw), (v_in, v_own), (q_in, q_own), (g_in, g_own)))
    ]
    for c in loads:
        c.start()
    get_pos.start()
    get_counts.start()

    def remote(src, dst, ss, rs, **where):
        return pltpu.make_async_remote_copy(
            src_ref=src, dst_ref=dst, send_sem=ss, recv_sem=rs, device_id=where, device_id_type=MESH
        )

    def columns(i, width):
        return pl.ds(pl.multiple_of(i * width, width), width)

    kv_in = (k_own, v_own)

    def kv_copy(i, src, to):
        return remote(
            kv_in[i].at[:, columns(to, WIDTH)], kv_ring.at[i, 3, src], sem_kv_s.at[i, to], sem_kv_r.at[i, src], seq=to
        )

    def wide_copy(arr, got, ss, rs, src, to):
        return remote(arr.at[:, columns(to, 1024)], got.at[src], ss.at[to], rs.at[src], seq=to)

    q_copy = functools.partial(wide_copy, q_own, q_got, sem_q_s, sem_q_r)
    g_copy = functools.partial(wide_copy, g_own, g_got, sem_g_s, sem_g_r)
    others = [lax.rem(me + d, NSEQ) for d in range(1, NSEQ)]
    own_kv = [
        pltpu.make_async_copy(kv_in[i].at[:, columns(me, WIDTH)], kv_ring.at[i, 3, me], sem_kv_r.at[i, me])
        for i in range(2)
    ]
    own_q = pltpu.make_async_copy(q_own.at[:, columns(me, 1024)], q_got.at[me], sem_q_r.at[me])
    own_g = pltpu.make_async_copy(g_own.at[:, columns(me, 1024)], g_got.at[me], sem_g_r.at[me])
    get_pos.wait()
    for s in range(NSEQ):
        for r in range(ROWS):
            at = pos[s * CAP + mz * ROWS + r].astype(F32)
            pos_row[s, r : r + 1, :] = jnp.full((1, WIDTH), at, F32)
    lane = lax.broadcasted_iota(jnp.int32, (1, WIDTH), 1)
    upper = lane >= WIDTH // 2
    half = jnp.where(upper, lane - WIDTH // 2, lane).astype(F32)
    freq = jnp.float32(ROPE_BASE) ** (-(half * 2.0 / WIDTH))
    for s in range(NSEQ):
        angle = pos_row[s] * freq
        cos[s] = jnp.cos(angle)
        sine = jnp.sin(angle)
        sin[s] = jnp.where(upper, sine, -sine)
    for c in loads:
        c.wait()
    for g in range(GROUPS):
        cols = slice(g * WIDTH, (g + 1) * WIDTH)
        k_own[:, cols] = rope(k_raw[:, cols].astype(F32), cos[me], sin[me]).astype(BF16)
    pl.semaphore_wait(barrier, NSEQ - 1 + 4)
    for i in range(2):
        for to in others:
            kv_copy(i, me, to).start()
        own_kv[i].start()
    for to in others:
        q_copy(me, to).start()
    own_q.start()
    for to in others:
        g_copy(me, to).start()
    own_g.start()

    get_counts.wait()
    row_in = lax.broadcasted_iota(jnp.int32, (ROWS, WIDTH), 0) + mz * ROWS
    for h in range(HEADS):
        limit[h * ROWS : (h + 1) * ROWS, :] = row_in
    lane = lax.broadcasted_iota(jnp.int32, (8, WIDEST), 1)
    for q in range(LAST + 1):
        ids = jnp.full((8, WIDEST), BIG, jnp.int32)
        for w, o in enumerate(OFFSETS[q]):
            first = away(o) * ROWS
            for s in range(NSEQ):
                lo = s * STEP[q] + w * ROWS
                at = lane - lo + first
                here = (lane >= lo) & (lane < lo + ROWS) & (at < counts[s])
                ids = jnp.where(here, at + s * CAP, ids)
        slot[q] = ids

    def ag_copy(i, dr, t):
        sign = 1 - 2 * dr
        far = t == 3
        src = -2 * sign if far else -sign * t
        dst = 4 if far else -sign * (t + 1)
        return remote(
            kv_ring.at[i, 3 + src], kv_ring.at[i, 3 + dst], sem_ag_s.at[i, dr, t], sem_ag_r.at[i, dr, t],
            head=away(2 * sign if far else sign),
        )

    def ag_all(t):
        return [(i, dr) for i in range(2) for dr in range(2) if t < 3 or i == dr]

    for i in range(2):
        own_kv[i].wait()
        for src in others:
            kv_copy(i, src, src).wait_recv()
        for dr in range(2):
            ag_copy(i, dr, 0).start()
    for whole in (k_all, v_all):
        for q in range(LAST + 1):
            rest = WIDEST - NSEQ * STEP[q]
            whole[q, NSEQ * STEP[q] : WIDEST, :] = jnp.zeros((rest, WIDTH), BF16)

    def place_q(s):
        for h in range(HEADS):
            x = rope(q_got[s, :, h * WIDTH : (h + 1) * WIDTH].astype(F32), cos[s], sin[s])
            stage[h * ROWS : (h + 1) * ROWS, :] = x
        q_all[s] = stage[...].astype(BF16)

    def place_g(s):
        for h in range(HEADS):
            stage[h * ROWS : (h + 1) * ROWS, :] = g_got[s, :, h * WIDTH : (h + 1) * WIDTH].astype(F32)
        g_all[s] = stage[...].astype(BF16)

    def out_copy(send, out, ss, rs, src, to):
        return remote(send.at[to], out.at[:, columns(src, 1024)], ss.at[to], rs.at[src], seq=to)

    o_copy = functools.partial(out_copy, o_send, att_out, sem_o_s, sem_o_r)
    dq_copy = functools.partial(out_copy, dq_send, dq_out, sem_dq_s, sem_dq_r)

    def own_out(send, out, rs):
        return pltpu.make_async_copy(send.at[me], out.at[:, columns(me, 1024)], rs.at[me])

    def send_back(own, copy):
        for to in others:
            copy(me, to).start()
        own.start()

    def line_up(i, whole, q):
        for w, o in enumerate(OFFSETS[q]):
            for s in range(NSEQ):
                lo = s * STEP[q] + w * ROWS
                pair_stage[lo : lo + ROWS, :] = kv_ring[i, 3 + o, s].astype(F32)
        whole[q, 0 : NSEQ * STEP[q], :] = pair_stage[0 : NSEQ * STEP[q], :].astype(BF16)

    def weigh(q):
        line_up(0, k_all, q)
        for s in reversed(range(NSEQ)):
            lim = limit[...] + s * CAP
            sc = dot_nt(q_all[s], k_all[q, 0 : WIDE[q][s], :])
            top = jnp.full((CAP, WIDTH), -1e30, F32)
            xs = []
            for lo in range(0, WIDE[q][s], WIDTH):
                x = jnp.where(slot[q, 0:1, lo : lo + WIDTH] <= lim, sc[:, lo : lo + WIDTH], -1e30)
                top = jnp.maximum(top, x)
                xs.append(x)
            top = jnp.broadcast_to(jnp.max(top, 1, keepdims=True), (CAP, WIDTH))
            if q > 0:
                before = top_all[q - 1, s]
                top = jnp.maximum(top, before)
            top_all[q, s] = top
            total = jnp.zeros((CAP, WIDTH), F32)
            for n, x in enumerate(xs):
                w = jnp.exp2((x - top) * SCALE2)
                w_all[:, START[q][s] + n * WIDTH : START[q][s] + (n + 1) * WIDTH] = w
                total = total + w
            if q > 0:
                total = total + sum_all[s] * jnp.exp2((before - top) * SCALE2)
            sum_all[s] = total

    def gather(q):
        line_up(1, v_all, q)
        for s in reversed(range(NSEQ)):
            w = w_all[:, START[q][s] : START[q][s] + WIDE[q][s]].astype(BF16)
            acc = dot_nn(w, v_all[q, 0 : WIDE[q][s], :])
            if q > 0:
                acc = acc + acc_all[s] * jnp.exp2((top_all[q - 1, s] - top_all[q, s]) * SCALE2)
            if q < LAST:
                acc_all[s] = acc
            else:
                live = (limit[...] < counts[s]).astype(F32)
                inv = live / jnp.sum(sum_all[s], 1, keepdims=True)
                inv_all[s] = inv
                att = (acc * inv).astype(BF16)
                att_all[s] = att

    def arrive(t, i):
        for dr in range(2):
            if t < 3 or i == dr:
                ag_copy(i, dr, t).wait_recv()
                if t < 2:
                    ag_copy(i, dr, t + 1).start()
                if t == 1 and i == dr:
                    ag_copy(i, dr, 3).start()

    def q_step(s, carry):
        place_q(s)
        return carry

    arrive(0, 0)
    arrive(0, 1)
    own_q.wait()
    for src in others:
        q_copy(src, src).wait_recv()
    lax.fori_loop(0, NSEQ, q_step, 0)
    weigh(0)
    gather(0)
    arrive(1, 0)
    weigh(1)
    arrive(1, 1)
    gather(1)
    weigh(2)
    gather(2)
    arrive(2, 0)
    weigh(3)
    arrive(2, 1)
    gather(3)

    def g_step(s, carry):
        place_g(s)
        return carry

    own_g.wait()
    for src in others:
        g_copy(src, src).wait_recv()
    lax.fori_loop(0, NSEQ, g_step, 0)
    arrive(3, 0)
    weigh(4)
    arrive(3, 1)
    gather(4)

    def backward(q):
        for s in reversed(range(NSEQ)):
            width = WIDE[q][s]
            qb = q_all[s]
            gb = g_all[s]
            scale = inv_all[s]
            if q == LAST:
                delta = jnp.sum(gb.astype(F32) * att_all[s].astype(F32), 1, keepdims=True)
                delta = jnp.broadcast_to(delta, (CAP, WIDTH))
                delta_all[s] = delta
            else:
                delta = delta_all[s]
                scale = scale * jnp.exp2((top_all[q, s] - top_all[LAST, s]) * SCALE2)
            dp = dot_nt(gb, v_all[q, 0:width, :])
            ps, ds = [], []
            for lo in range(0, width, WIDTH):
                at = START[q][s] + lo
                p = w_all[:, at : at + WIDTH] * scale
                ps.append(p.astype(BF16))
                d = (p * (dp[:, lo : lo + WIDTH] - delta)).astype(BF16)
                ds_all[:, at : at + WIDTH] = d
                ds.append(d)
            dv = dot_tn(gb, jnp.concatenate(ps, 1))
            dk = dot_tn(qb, jnp.concatenate(ds, 1))
            if s == NSEQ - 1:
                dv_turned[:, 0:width] = dv
                dk_turned[:, 0:width] = dk
            else:
                dv_turned[:, 0:width] += dv
                dk_turned[:, 0:width] += dk
        width = WIDE[q][NSEQ - 1]
        dk_acc[q, 0:width, :] = dk_turned[:, 0:width].T
        dv_acc[q, 0:width, :] = dv_turned[:, 0:width].T

    accs = (dk_acc, dv_acc)

    def own_part(i, o, s):
        q, w = PLACE[o]
        lo = s * STEP[q] + w * ROWS
        return accs[i][q, lo : lo + ROWS, :]

    def rs_copy(kind, dr, i):
        sign = 1 - 2 * dr
        return remote(
            rs_out.at[kind, dr, i], rs_in.at[kind, dr, i], sem_rs_s.at[kind, dr, i], sem_rs_r.at[kind, dr, i],
            head=away(2 * sign if kind in (FAR, SECOND) else sign),
        )

    def rs_kinds(kind, dr):
        return [i for i in range(2) if kind != FAR or i == dr]

    def scatter(kind):
        for i, dr in [(i, dr) for i in range(2) for dr in range(2) if kind != FAR or i == dr]:
            o = 4 if kind == FAR else (1 - 2 * dr) * DISTANCE[kind]
            adds = []
            if kind == SECOND:
                adds = [THIRD] + ([FAR] if i == dr else [])
            for a in adds:
                rs_copy(a, dr, i).wait_recv()
            for s in range(NSEQ):
                x = own_part(i, o, s)
                for a in adds:
                    x = x + rs_in[a, dr, i, s].astype(F32)
                rs_out[kind, dr, i, s] = x.astype(BF16)
            rs_copy(kind, dr, i).start()

    backward(4)
    scatter(FAR)
    backward(3)
    scatter(THIRD)
    for s in range(NSEQ):
        att = att_all[s].astype(F32)
        for h in range(HEADS):
            o_send[s, :, h * WIDTH : (h + 1) * WIDTH] = att[h * ROWS : (h + 1) * ROWS].astype(BF16)
    send_back(own_out(o_send, att_out, sem_o_r), o_copy)
    backward(1)
    scatter(FIRST)
    backward(2)
    scatter(SECOND)
    backward(0)

    for s in reversed(range(NSEQ)):
        dq = jnp.zeros((CAP, WIDTH), F32)
        for q in range(LAST + 1):
            d = ds_all[:, START[q][s] : START[q][s] + WIDE[q][s]]
            dq = dq + dot_nn(d, k_all[q, 0 : WIDE[q][s], :])
        dq = dq * SCALE
        for h in range(HEADS):
            x = rope_t(dq[h * ROWS : (h + 1) * ROWS], cos[s], sin[s])
            dq_send[s, :, h * WIDTH : (h + 1) * WIDTH] = x.astype(BF16)
    send_back(own_out(dq_send, dq_out, sem_dq_r), dq_copy)

    for to in others:
        for i in range(2):
            kv_copy(i, me, to).wait_send()
        q_copy(me, to).wait_send()
        g_copy(me, to).wait_send()
        o_copy(me, to).wait_send()
    for t in range(4):
        for i, dr in ag_all(t):
            ag_copy(i, dr, t).wait_send()
    for kind in (FAR, THIRD, FIRST):
        for dr in range(2):
            for i in rs_kinds(kind, dr):
                rs_copy(kind, dr, i).wait_send()
    own_out(o_send, att_out, sem_o_r).wait()
    for src in others:
        o_copy(src, me).wait_recv()

    kv_out = (dk_out, dv_out)

    def back_copy(i, src, to):
        return remote(
            kv_send.at[i, to], kv_out[i].at[:, columns(src, WIDTH)], sem_b_s.at[i, to], sem_b_r.at[i, src], seq=to
        )

    own_back = [
        pltpu.make_async_copy(kv_send.at[i, me], kv_out[i].at[:, columns(me, WIDTH)], sem_b_r.at[i, me])
        for i in range(2)
    ]
    for i in range(2):
        ends = [(kind, dr) for kind in (FIRST, SECOND) for dr in range(2)]
        for kind, dr in ends:
            rs_copy(kind, dr, i).wait_recv()
        for s in range(NSEQ):
            x = own_part(i, 0, s)
            for kind, dr in ends:
                x = x + rs_in[kind, dr, i, s].astype(F32)
            if i == 0:
                x = rope_t(x * SCALE, cos[s], sin[s])
            kv_send[i, s] = x.astype(BF16)
        send_back(own_back[i], functools.partial(back_copy, i))

    for dr in range(2):
        for i in range(2):
            rs_copy(SECOND, dr, i).wait_send()
    own_out(dq_send, dq_out, sem_dq_r).wait()
    for src in others:
        dq_copy(src, me).wait_recv()
    for to in others:
        dq_copy(me, to).wait_send()
    for i in range(2):
        own_back[i].wait()
        for src in others:
            back_copy(i, src, me).wait_recv()
        for to in others:
            back_copy(i, me, to).wait_send()


def deliver(*refs):
    held, load_sem, store_sem = refs[8:12], refs[12], refs[13]
    loads = [pltpu.make_async_copy(refs[i], held[i], load_sem.at[i]) for i in range(4)]
    stores = [pltpu.make_async_copy(held[i], refs[i + 4], store_sem.at[i]) for i in range(4)]
    for c in loads:
        c.start()
    for i in range(4):
        loads[i].wait()
        stores[i].start()
    for c in stores:
        c.wait()


def shards(queries, routed_keys, routed_values, output_gradient, positions, counts):
    anywhere = pl.BlockSpec(memory_space=pl.ANY)
    dma = pltpu.SemaphoreType.DMA
    out = jax.ShapeDtypeStruct
    wide = (ROWS, QUERY_HEADS * WIDTH)
    slim = (ROWS, GROUPS * WIDTH)
    results = [out(wide, BF16), out(wide, BF16), out(slim, BF16), out(slim, BF16)]
    by_shard = pltpu.VMEM((NSEQ, CAP, WIDTH), F32)
    found = pl.pallas_call(
        kernel,
        out_shape=results,
        in_specs=[anywhere] * 6,
        out_specs=[anywhere] * 4,
        scratch_shapes=[
            pltpu.SMEM((SLOTS,), jnp.int32),
            pltpu.SMEM((NSEQ,), jnp.int32),
            pltpu.VMEM((NSEQ, ROWS, WIDTH), F32),
            pltpu.VMEM((NSEQ, ROWS, WIDTH), F32),
            pltpu.VMEM((NSEQ, ROWS, WIDTH), F32),
            pltpu.VMEM(wide, BF16),
            pltpu.VMEM(wide, BF16),
            pltpu.VMEM(slim, BF16),
            pltpu.VMEM(slim, BF16),
            pltpu.VMEM(slim, BF16),
            pltpu.VMEM((NSEQ, ROWS, HEADS * WIDTH), BF16),
            pltpu.VMEM((NSEQ, ROWS, HEADS * WIDTH), BF16),
            pltpu.VMEM((2, NZ, NSEQ, ROWS, WIDTH), BF16),
            pltpu.VMEM((CAP, WIDTH), F32),
            pltpu.VMEM((NSEQ, CAP, WIDTH), BF16),
            pltpu.VMEM((NSEQ, CAP, WIDTH), BF16),
            pltpu.VMEM((NSEQ * max(STEP), WIDTH), F32),
            pltpu.VMEM((LAST + 1, WIDEST, WIDTH), BF16),
            pltpu.VMEM((LAST + 1, WIDEST, WIDTH), BF16),
            pltpu.VMEM((LAST + 1, 8, WIDEST), jnp.int32),
            pltpu.VMEM((CAP, WIDTH), jnp.int32),
            pltpu.VMEM((CAP, STORE), F32),
            pltpu.VMEM((CAP, STORE), BF16),
            pltpu.VMEM((LAST + 1, NSEQ, CAP, WIDTH), F32),
            by_shard,
            by_shard,
            by_shard,
            by_shard,
            pltpu.VMEM((NSEQ, CAP, WIDTH), BF16),
            pltpu.VMEM((LAST + 1, WIDEST, WIDTH), F32),
            pltpu.VMEM((LAST + 1, WIDEST, WIDTH), F32),
            pltpu.VMEM((WIDTH, WIDEST), F32),
            pltpu.VMEM((WIDTH, WIDEST), F32),
            pltpu.VMEM((NSEQ, ROWS, HEADS * WIDTH), BF16),
            pltpu.VMEM((NSEQ, ROWS, HEADS * WIDTH), BF16),
            pltpu.VMEM((4, 2, 2, NSEQ, ROWS, WIDTH), BF16),
            pltpu.VMEM((4, 2, 2, NSEQ, ROWS, WIDTH), BF16),
            pltpu.VMEM((2, NSEQ, ROWS, WIDTH), BF16),
            dma((2,)), dma((4,)),
            dma((2, NSEQ)), dma((2, NSEQ)), dma((NSEQ,)), dma((NSEQ,)), dma((NSEQ,)), dma((NSEQ,)),
            dma((2, 2, 4)), dma((2, 2, 4)),
            dma((NSEQ,)), dma((NSEQ,)), dma((NSEQ,)), dma((NSEQ,)),
            dma((4, 2, 2)), dma((4, 2, 2)), dma((2, NSEQ)), dma((2, NSEQ)),
        ],
        compiler_params=pltpu.CompilerParams(
            collective_id=0, has_side_effects=True, vmem_limit_bytes=60 * 2**20
        ),
        cost_estimate=pl.CostEstimate(flops=5 * 10**9, bytes_accessed=4 * 10**6, transcendentals=3 * 10**6),
    )(positions, counts, queries, routed_keys, routed_values, output_gradient)
    return pl.pallas_call(
        deliver,
        out_shape=results,
        in_specs=[anywhere] * 4,
        out_specs=[anywhere] * 4,
        scratch_shapes=[
            pltpu.VMEM(wide, BF16), pltpu.VMEM(wide, BF16), pltpu.VMEM(slim, BF16), pltpu.VMEM(slim, BF16),
            dma((4,)), dma((4,)),
        ],
    )(*found)


def solution(mesh):
    rows = P(("dp", "seq", "head"), None)
    return jax.shard_map(
        shards, mesh=mesh, in_specs=(rows, rows, rows, rows, P("dp"), P("dp")), out_specs=(rows,) * 4, check_vma=False
    )
```

```python
import functools

import jax
import jax.numpy as jnp
import numpy as np
from jax import lax
from jax.experimental import pallas as pl
from jax.experimental.pallas import tpu as pltpu
from jax.sharding import PartitionSpec as P

QUERY_HEADS = 64
GROUPS = 8
HEADS = 8
WIDTH = 128
NSEQ = 8
NZ = 8
ROWS = 36
CAP = 288
SLOTS = 2304
WIDEST = 640
ROPE_BASE = 500000.0
BIG = 1 << 20
SCALE = 1.0 / np.sqrt(128.0)
SCALE2 = float(SCALE * np.log2(np.e))
MESH = pl.DeviceIdType.MESH
F32 = jnp.float32
BF16 = jnp.bfloat16


def dot_nt(a, b):
    return lax.dot_general(a, b, (((1,), (1,)), ((), ())), preferred_element_type=F32)


def dot_tn(a, b):
    return lax.dot_general(a, b, (((0,), (0,)), ((), ())), preferred_element_type=F32)


def dot_nn(a, b):
    return jnp.dot(a, b, preferred_element_type=F32)


def roll_half(x):
    return pltpu.roll(x, WIDTH // 2, 1)


def rope(x, cos, sin):
    return x * cos + roll_half(x) * sin


def rope_t(x, cos, sin):
    return x * cos - roll_half(x) * sin


OFFSETS = ((0,), (1, -1), (2, -2), (3, -3), (4,))
LAST = len(OFFSETS) - 1
PLACE = {o: (q, w) for q, group in enumerate(OFFSETS) for w, o in enumerate(group)}
STEP = tuple(ROWS * len(group) for group in OFFSETS)
WIDE = tuple(tuple(-(-step * (s + 1) // WIDTH) * WIDTH for s in range(NSEQ)) for step in STEP)
START, STORE = [], 0
for _wide in WIDE:
    START.append([])
    for _w in _wide:
        START[-1].append(STORE)
        STORE += _w
FAR, THIRD, SECOND, FIRST = range(4)
DISTANCE = (4, 3, 2, 1)


def kernel(
    pos_in, counts_in, q_in, k_in, v_in, g_in,
    att_out, dq_out, dk_out, dv_out,
    pos, counts, pos_row, cos, sin, q_own, g_own, k_raw, k_own, v_own,
    q_got, g_got, kv_ring, stage, q_all, g_all, pair_stage, k_all, v_all,
    slot, limit, w_all, ds_all, top_all, sum_all, acc_all, inv_all, delta_all, att_all,
    dk_acc, dv_acc, dk_turned, dv_turned, o_send, dq_send, rs_out, rs_in, kv_send,
    sem_p, sem_in, sem_kv_s, sem_kv_r, sem_q_s, sem_q_r, sem_g_s, sem_g_r, sem_ag_s, sem_ag_r,
    sem_o_s, sem_o_r, sem_dq_s, sem_dq_r, sem_rs_s, sem_rs_r, sem_b_s, sem_b_r,
):
    me = lax.axis_index("seq")
    mz = lax.axis_index("head")

    def away(o):
        return lax.rem(mz + (o + NZ), NZ)

    barrier = pltpu.get_barrier_semaphore()
    for d in range(1, NSEQ):
        pl.semaphore_signal(barrier, inc=1, device_id={"seq": lax.rem(me + d, NSEQ)}, device_id_type=MESH)
    for o in (1, -1, 2, -2):
        pl.semaphore_signal(barrier, inc=1, device_id={"head": away(o)}, device_id_type=MESH)
    get_pos = pltpu.make_async_copy(pos_in, pos, sem_p.at[0])
    get_counts = pltpu.make_async_copy(counts_in, counts, sem_p.at[1])
    loads = [
        pltpu.make_async_copy(src, dst, sem_in.at[i])
        for i, (src, dst) in enumerate(((k_in, k_raw), (v_in, v_own), (q_in, q_own), (g_in, g_own)))
    ]
    for c in loads:
        c.start()
    get_pos.start()
    get_counts.start()

    def remote(src, dst, ss, rs, **where):
        return pltpu.make_async_remote_copy(
            src_ref=src, dst_ref=dst, send_sem=ss, recv_sem=rs, device_id=where, device_id_type=MESH
        )

    def columns(i, width):
        return pl.ds(pl.multiple_of(i * width, width), width)

    kv_in = (k_own, v_own)

    def kv_copy(i, src, to):
        return remote(
            kv_in[i].at[:, columns(to, WIDTH)], kv_ring.at[i, 3, src], sem_kv_s.at[i, to], sem_kv_r.at[i, src], seq=to
        )

    def wide_copy(arr, got, ss, rs, src, to):
        return remote(arr.at[:, columns(to, 1024)], got.at[src], ss.at[to], rs.at[src], seq=to)

    q_copy = functools.partial(wide_copy, q_own, q_got, sem_q_s, sem_q_r)
    g_copy = functools.partial(wide_copy, g_own, g_got, sem_g_s, sem_g_r)
    others = [lax.rem(me + d, NSEQ) for d in range(1, NSEQ)]
    own_kv = [
        pltpu.make_async_copy(kv_in[i].at[:, columns(me, WIDTH)], kv_ring.at[i, 3, me], sem_kv_r.at[i, me])
        for i in range(2)
    ]
    own_q = pltpu.make_async_copy(q_own.at[:, columns(me, 1024)], q_got.at[me], sem_q_r.at[me])
    own_g = pltpu.make_async_copy(g_own.at[:, columns(me, 1024)], g_got.at[me], sem_g_r.at[me])
    get_pos.wait()
    for s in range(NSEQ):
        for r in range(ROWS):
            at = pos[s * CAP + mz * ROWS + r].astype(F32)
            pos_row[s, r : r + 1, :] = jnp.full((1, WIDTH), at, F32)
    lane = lax.broadcasted_iota(jnp.int32, (1, WIDTH), 1)
    upper = lane >= WIDTH // 2
    half = jnp.where(upper, lane - WIDTH // 2, lane).astype(F32)
    freq = jnp.float32(ROPE_BASE) ** (-(half * 2.0 / WIDTH))
    for s in range(NSEQ):
        angle = pos_row[s] * freq
        cos[s] = jnp.cos(angle)
        sine = jnp.sin(angle)
        sin[s] = jnp.where(upper, sine, -sine)
    for c in loads:
        c.wait()
    for g in range(GROUPS):
        cols = slice(g * WIDTH, (g + 1) * WIDTH)
        k_own[:, cols] = rope(k_raw[:, cols].astype(F32), cos[me], sin[me]).astype(BF16)
    pl.semaphore_wait(barrier, NSEQ - 1 + 4)
    for i in range(2):
        for to in others:
            kv_copy(i, me, to).start()
        own_kv[i].start()
    for to in others:
        q_copy(me, to).start()
    own_q.start()
    for to in others:
        g_copy(me, to).start()
    own_g.start()

    get_counts.wait()
    row_in = lax.broadcasted_iota(jnp.int32, (ROWS, WIDTH), 0) + mz * ROWS
    for h in range(HEADS):
        limit[h * ROWS : (h + 1) * ROWS, :] = row_in
    lane = lax.broadcasted_iota(jnp.int32, (8, WIDEST), 1)
    for q in range(LAST + 1):
        ids = jnp.full((8, WIDEST), BIG, jnp.int32)
        for w, o in enumerate(OFFSETS[q]):
            first = away(o) * ROWS
            for s in range(NSEQ):
                lo = s * STEP[q] + w * ROWS
                at = lane - lo + first
                here = (lane >= lo) & (lane < lo + ROWS) & (at < counts[s])
                ids = jnp.where(here, at + s * CAP, ids)
        slot[q] = ids

    def ag_copy(i, dr, t):
        sign = 1 - 2 * dr
        far = t == 3
        src = -2 * sign if far else -sign * t
        dst = 4 if far else -sign * (t + 1)
        return remote(
            kv_ring.at[i, 3 + src], kv_ring.at[i, 3 + dst], sem_ag_s.at[i, dr, t], sem_ag_r.at[i, dr, t],
            head=away(2 * sign if far else sign),
        )

    def ag_all(t):
        return [(i, dr) for i in range(2) for dr in range(2) if t < 3 or i == dr]

    for i in range(2):
        own_kv[i].wait()
        for src in others:
            kv_copy(i, src, src).wait_recv()
        for dr in range(2):
            ag_copy(i, dr, 0).start()
    for whole in (k_all, v_all):
        for q in range(LAST + 1):
            rest = WIDEST - NSEQ * STEP[q]
            whole[q, NSEQ * STEP[q] : WIDEST, :] = jnp.zeros((rest, WIDTH), BF16)

    def place_q(s):
        for h in range(HEADS):
            x = rope(q_got[s, :, h * WIDTH : (h + 1) * WIDTH].astype(F32), cos[s], sin[s])
            stage[h * ROWS : (h + 1) * ROWS, :] = x
        q_all[s] = stage[...].astype(BF16)

    def place_g(s):
        for h in range(HEADS):
            stage[h * ROWS : (h + 1) * ROWS, :] = g_got[s, :, h * WIDTH : (h + 1) * WIDTH].astype(F32)
        g_all[s] = stage[...].astype(BF16)

    def out_copy(send, out, ss, rs, src, to):
        return remote(send.at[to], out.at[:, columns(src, 1024)], ss.at[to], rs.at[src], seq=to)

    o_copy = functools.partial(out_copy, o_send, att_out, sem_o_s, sem_o_r)
    dq_copy = functools.partial(out_copy, dq_send, dq_out, sem_dq_s, sem_dq_r)

    def own_out(send, out, rs):
        return pltpu.make_async_copy(send.at[me], out.at[:, columns(me, 1024)], rs.at[me])

    def send_back(own, copy):
        for to in others:
            copy(me, to).start()
        own.start()

    def line_up(i, whole, q):
        for w, o in enumerate(OFFSETS[q]):
            for s in range(NSEQ):
                lo = s * STEP[q] + w * ROWS
                pair_stage[lo : lo + ROWS, :] = kv_ring[i, 3 + o, s].astype(F32)
        whole[q, 0 : NSEQ * STEP[q], :] = pair_stage[0 : NSEQ * STEP[q], :].astype(BF16)

    def weigh(q):
        line_up(0, k_all, q)
        for s in reversed(range(NSEQ)):
            lim = limit[...] + s * CAP
            sc = dot_nt(q_all[s], k_all[q, 0 : WIDE[q][s], :])
            top = jnp.full((CAP, WIDTH), -1e30, F32)
            xs = []
            for lo in range(0, WIDE[q][s], WIDTH):
                x = jnp.where(slot[q, 0:1, lo : lo + WIDTH] <= lim, sc[:, lo : lo + WIDTH], -1e30)
                top = jnp.maximum(top, x)
                xs.append(x)
            top = jnp.broadcast_to(jnp.max(top, 1, keepdims=True), (CAP, WIDTH))
            if q > 0:
                before = top_all[q - 1, s]
                top = jnp.maximum(top, before)
            top_all[q, s] = top
            total = jnp.zeros((CAP, WIDTH), F32)
            for n, x in enumerate(xs):
                w = jnp.exp2((x - top) * SCALE2)
                w_all[:, START[q][s] + n * WIDTH : START[q][s] + (n + 1) * WIDTH] = w
                total = total + w
            if q > 0:
                total = total + sum_all[s] * jnp.exp2((before - top) * SCALE2)
            sum_all[s] = total

    def gather(q):
        line_up(1, v_all, q)
        for s in reversed(range(NSEQ)):
            w = w_all[:, START[q][s] : START[q][s] + WIDE[q][s]].astype(BF16)
            acc = dot_nn(w, v_all[q, 0 : WIDE[q][s], :])
            if q > 0:
                acc = acc + acc_all[s] * jnp.exp2((top_all[q - 1, s] - top_all[q, s]) * SCALE2)
            if q < LAST:
                acc_all[s] = acc
            else:
                live = (limit[...] < counts[s]).astype(F32)
                inv = live / jnp.sum(sum_all[s], 1, keepdims=True)
                inv_all[s] = inv
                att = (acc * inv).astype(BF16)
                att_all[s] = att

    def arrive(t, i):
        for dr in range(2):
            if t < 3 or i == dr:
                ag_copy(i, dr, t).wait_recv()
                if t < 2:
                    ag_copy(i, dr, t + 1).start()
                if t == 1 and i == dr:
                    ag_copy(i, dr, 3).start()

    def q_step(s, carry):
        place_q(s)
        return carry

    arrive(0, 0)
    arrive(0, 1)
    own_q.wait()
    for src in others:
        q_copy(src, src).wait_recv()
    lax.fori_loop(0, NSEQ, q_step, 0)
    weigh(0)
    gather(0)
    arrive(1, 0)
    weigh(1)
    arrive(1, 1)
    gather(1)
    weigh(2)
    gather(2)
    arrive(2, 0)
    weigh(3)
    arrive(2, 1)
    gather(3)

    def g_step(s, carry):
        place_g(s)
        return carry

    own_g.wait()
    for src in others:
        g_copy(src, src).wait_recv()
    lax.fori_loop(0, NSEQ, g_step, 0)
    arrive(3, 0)
    weigh(4)
    arrive(3, 1)
    gather(4)

    def backward(q):
        for s in reversed(range(NSEQ)):
            width = WIDE[q][s]
            qb = q_all[s]
            gb = g_all[s]
            scale = inv_all[s]
            if q == LAST:
                delta = jnp.sum(gb.astype(F32) * att_all[s].astype(F32), 1, keepdims=True)
                delta = jnp.broadcast_to(delta, (CAP, WIDTH))
                delta_all[s] = delta
            else:
                delta = delta_all[s]
                scale = scale * jnp.exp2((top_all[q, s] - top_all[LAST, s]) * SCALE2)
            dp = dot_nt(gb, v_all[q, 0:width, :])
            ps, ds = [], []
            for lo in range(0, width, WIDTH):
                at = START[q][s] + lo
                p = w_all[:, at : at + WIDTH] * scale
                ps.append(p.astype(BF16))
                d = (p * (dp[:, lo : lo + WIDTH] - delta)).astype(BF16)
                ds_all[:, at : at + WIDTH] = d
                ds.append(d)
            dv = dot_tn(gb, jnp.concatenate(ps, 1))
            dk = dot_tn(qb, jnp.concatenate(ds, 1))
            if s == NSEQ - 1:
                dv_turned[:, 0:width] = dv
                dk_turned[:, 0:width] = dk
            else:
                dv_turned[:, 0:width] += dv
                dk_turned[:, 0:width] += dk
        width = WIDE[q][NSEQ - 1]
        dk_acc[q, 0:width, :] = dk_turned[:, 0:width].T
        dv_acc[q, 0:width, :] = dv_turned[:, 0:width].T

    accs = (dk_acc, dv_acc)

    def own_part(i, o, s):
        q, w = PLACE[o]
        lo = s * STEP[q] + w * ROWS
        return accs[i][q, lo : lo + ROWS, :]

    def rs_copy(kind, dr, i):
        sign = 1 - 2 * dr
        return remote(
            rs_out.at[kind, dr, i], rs_in.at[kind, dr, i], sem_rs_s.at[kind, dr, i], sem_rs_r.at[kind, dr, i],
            head=away(2 * sign if kind in (FAR, SECOND) else sign),
        )

    def rs_kinds(kind, dr):
        return [i for i in range(2) if kind != FAR or i == dr]

    def scatter(kind):
        for i, dr in [(i, dr) for i in range(2) for dr in range(2) if kind != FAR or i == dr]:
            o = 4 if kind == FAR else (1 - 2 * dr) * DISTANCE[kind]
            adds = []
            if kind == SECOND:
                adds = [THIRD] + ([FAR] if i == dr else [])
            for a in adds:
                rs_copy(a, dr, i).wait_recv()
            for s in range(NSEQ):
                x = own_part(i, o, s)
                for a in adds:
                    x = x + rs_in[a, dr, i, s].astype(F32)
                rs_out[kind, dr, i, s] = x.astype(BF16)
            rs_copy(kind, dr, i).start()

    backward(4)
    scatter(FAR)
    backward(3)
    scatter(THIRD)
    for s in range(NSEQ):
        att = att_all[s].astype(F32)
        for h in range(HEADS):
            o_send[s, :, h * WIDTH : (h + 1) * WIDTH] = att[h * ROWS : (h + 1) * ROWS].astype(BF16)
    send_back(own_out(o_send, att_out, sem_o_r), o_copy)
    backward(1)
    scatter(FIRST)
    backward(2)
    scatter(SECOND)
    backward(0)

    for s in reversed(range(NSEQ)):
        dq = jnp.zeros((CAP, WIDTH), F32)
        for q in range(LAST + 1):
            d = ds_all[:, START[q][s] : START[q][s] + WIDE[q][s]]
            dq = dq + dot_nn(d, k_all[q, 0 : WIDE[q][s], :])
        dq = dq * SCALE
        for h in range(HEADS):
            x = rope_t(dq[h * ROWS : (h + 1) * ROWS], cos[s], sin[s])
            dq_send[s, :, h * WIDTH : (h + 1) * WIDTH] = x.astype(BF16)
        if s in (6, 4, 2, 0):
            for to in (s + 1, s):

                @pl.when(me == to)
                def _():
                    own_out(dq_send, dq_out, sem_dq_r).start()

                @pl.when(me != to)
                def _():
                    dq_copy(me, to).start()

    for to in others:
        for i in range(2):
            kv_copy(i, me, to).wait_send()
        q_copy(me, to).wait_send()
        g_copy(me, to).wait_send()
        o_copy(me, to).wait_send()
    for t in range(4):
        for i, dr in ag_all(t):
            ag_copy(i, dr, t).wait_send()
    for kind in (FAR, THIRD, FIRST):
        for dr in range(2):
            for i in rs_kinds(kind, dr):
                rs_copy(kind, dr, i).wait_send()
    own_out(o_send, att_out, sem_o_r).wait()
    for src in others:
        o_copy(src, me).wait_recv()

    kv_out = (dk_out, dv_out)

    def back_copy(i, src, to):
        return remote(
            kv_send.at[i, to], kv_out[i].at[:, columns(src, WIDTH)], sem_b_s.at[i, to], sem_b_r.at[i, src], seq=to
        )

    own_back = [
        pltpu.make_async_copy(kv_send.at[i, me], kv_out[i].at[:, columns(me, WIDTH)], sem_b_r.at[i, me])
        for i in range(2)
    ]
    for i in range(2):
        ends = [(kind, dr) for kind in (FIRST, SECOND) for dr in range(2)]
        for kind, dr in ends:
            rs_copy(kind, dr, i).wait_recv()
        for s in range(NSEQ):
            x = own_part(i, 0, s)
            for kind, dr in ends:
                x = x + rs_in[kind, dr, i, s].astype(F32)
            if i == 0:
                x = rope_t(x * SCALE, cos[s], sin[s])
            kv_send[i, s] = x.astype(BF16)
        send_back(own_back[i], functools.partial(back_copy, i))

    for dr in range(2):
        for i in range(2):
            rs_copy(SECOND, dr, i).wait_send()
    own_out(dq_send, dq_out, sem_dq_r).wait()
    for src in others:
        dq_copy(src, me).wait_recv()
    for to in others:
        dq_copy(me, to).wait_send()
    for i in range(2):
        own_back[i].wait()
        for src in others:
            back_copy(i, src, me).wait_recv()
        for to in others:
            back_copy(i, me, to).wait_send()


def deliver(*refs):
    held, load_sem, store_sem = refs[8:12], refs[12], refs[13]
    loads = [pltpu.make_async_copy(refs[i], held[i], load_sem.at[i]) for i in range(4)]
    stores = [pltpu.make_async_copy(held[i], refs[i + 4], store_sem.at[i]) for i in range(4)]
    for c in loads:
        c.start()
    for i in range(4):
        loads[i].wait()
        stores[i].start()
    for c in stores:
        c.wait()


def shards(queries, routed_keys, routed_values, output_gradient, positions, counts):
    anywhere = pl.BlockSpec(memory_space=pl.ANY)
    dma = pltpu.SemaphoreType.DMA
    out = jax.ShapeDtypeStruct
    wide = (ROWS, QUERY_HEADS * WIDTH)
    slim = (ROWS, GROUPS * WIDTH)
    results = [out(wide, BF16), out(wide, BF16), out(slim, BF16), out(slim, BF16)]
    by_shard = pltpu.VMEM((NSEQ, CAP, WIDTH), F32)
    found = pl.pallas_call(
        kernel,
        out_shape=results,
        in_specs=[anywhere] * 6,
        out_specs=[anywhere] * 4,
        scratch_shapes=[
            pltpu.SMEM((SLOTS,), jnp.int32),
            pltpu.SMEM((NSEQ,), jnp.int32),
            pltpu.VMEM((NSEQ, ROWS, WIDTH), F32),
            pltpu.VMEM((NSEQ, ROWS, WIDTH), F32),
            pltpu.VMEM((NSEQ, ROWS, WIDTH), F32),
            pltpu.VMEM(wide, BF16),
            pltpu.VMEM(wide, BF16),
            pltpu.VMEM(slim, BF16),
            pltpu.VMEM(slim, BF16),
            pltpu.VMEM(slim, BF16),
            pltpu.VMEM((NSEQ, ROWS, HEADS * WIDTH), BF16),
            pltpu.VMEM((NSEQ, ROWS, HEADS * WIDTH), BF16),
            pltpu.VMEM((2, NZ, NSEQ, ROWS, WIDTH), BF16),
            pltpu.VMEM((CAP, WIDTH), F32),
            pltpu.VMEM((NSEQ, CAP, WIDTH), BF16),
            pltpu.VMEM((NSEQ, CAP, WIDTH), BF16),
            pltpu.VMEM((NSEQ * max(STEP), WIDTH), F32),
            pltpu.VMEM((LAST + 1, WIDEST, WIDTH), BF16),
            pltpu.VMEM((LAST + 1, WIDEST, WIDTH), BF16),
            pltpu.VMEM((LAST + 1, 8, WIDEST), jnp.int32),
            pltpu.VMEM((CAP, WIDTH), jnp.int32),
            pltpu.VMEM((CAP, STORE), F32),
            pltpu.VMEM((CAP, STORE), BF16),
            pltpu.VMEM((LAST + 1, NSEQ, CAP, WIDTH), F32),
            by_shard,
            by_shard,
            by_shard,
            by_shard,
            pltpu.VMEM((NSEQ, CAP, WIDTH), BF16),
            pltpu.VMEM((LAST + 1, WIDEST, WIDTH), F32),
            pltpu.VMEM((LAST + 1, WIDEST, WIDTH), F32),
            pltpu.VMEM((WIDTH, WIDEST), F32),
            pltpu.VMEM((WIDTH, WIDEST), F32),
            pltpu.VMEM((NSEQ, ROWS, HEADS * WIDTH), BF16),
            pltpu.VMEM((NSEQ, ROWS, HEADS * WIDTH), BF16),
            pltpu.VMEM((4, 2, 2, NSEQ, ROWS, WIDTH), BF16),
            pltpu.VMEM((4, 2, 2, NSEQ, ROWS, WIDTH), BF16),
            pltpu.VMEM((2, NSEQ, ROWS, WIDTH), BF16),
            dma((2,)), dma((4,)),
            dma((2, NSEQ)), dma((2, NSEQ)), dma((NSEQ,)), dma((NSEQ,)), dma((NSEQ,)), dma((NSEQ,)),
            dma((2, 2, 4)), dma((2, 2, 4)),
            dma((NSEQ,)), dma((NSEQ,)), dma((NSEQ,)), dma((NSEQ,)),
            dma((4, 2, 2)), dma((4, 2, 2)), dma((2, NSEQ)), dma((2, NSEQ)),
        ],
        compiler_params=pltpu.CompilerParams(
            collective_id=0, has_side_effects=True, vmem_limit_bytes=60 * 2**20
        ),
        cost_estimate=pl.CostEstimate(flops=5 * 10**9, bytes_accessed=4 * 10**6, transcendentals=3 * 10**6),
    )(positions, counts, queries, routed_keys, routed_values, output_gradient)
    return pl.pallas_call(
        deliver,
        out_shape=results,
        in_specs=[anywhere] * 4,
        out_specs=[anywhere] * 4,
        scratch_shapes=[
            pltpu.VMEM(wide, BF16), pltpu.VMEM(wide, BF16), pltpu.VMEM(slim, BF16), pltpu.VMEM(slim, BF16),
            dma((4,)), dma((4,)),
        ],
    )(*found)


def solution(mesh):
    rows = P(("dp", "seq", "head"), None)
    return jax.shard_map(
        shards, mesh=mesh, in_specs=(rows, rows, rows, rows, P("dp"), P("dp")), out_specs=(rows,) * 4, check_vma=False
    )
```
